128 devices in a mesh: ctx: 64 (over z_lo, y, x, core), batch: 2 (over z_hi).
Axes of the slice: x: 4, y: 4, z: 4 (z_hi: 2, z_lo: 2; z = z_hi * 2 + z_lo), core: 2. Of those that a mesh axis runs over, the one named last changes fastest.
Arguments:
- queries: bfloat16 [32768, 128], P(('batch', 'ctx')), parts along dimension 0, may hold values from -30 to 30
- keys: bfloat16 [32768, 128], P(('batch', 'ctx')), parts along dimension 0, may hold values from -30 to 30
- values: bfloat16 [32768, 128], P(('batch', 'ctx')), parts along dimension 0, may hold values from -6 to 6
- tan_queries: bfloat16 [32768, 128], P(('batch', 'ctx')), parts along dimension 0, may hold values from -6 to 6
- tan_keys: bfloat16 [32768, 128], P(('batch', 'ctx')), parts along dimension 0, may hold values from -6 to 6
- tan_values: bfloat16 [32768, 128], P(('batch', 'ctx')), parts along dimension 0, may hold values from -6 to 6
- segment_ids: int32 [32768], P(('batch', 'ctx')), parts along dimension 0, may hold values from 0 to 2, as said below
Outputs:
- attended: float32 [32768, 128], P(('batch', 'ctx')), parts along dimension 0
- tan_attended: float32 [32768, 128], P(('batch', 'ctx')), parts along dimension 0
The draws below stay inside these ranges and needn't reach their ends.
There are 2 independent parts, one for each index of `batch`. The reference program is written for one: setup_inputs(seed, part) draws one part's arguments, and reference() takes and returns one part's arrays. A program takes and returns all parts, laid end to end along the dimension named above; each array names one. Nothing has to cross between parts.
Inputs may be any that keep to these rules, and one draw needn't show every extreme that they name: `segment_ids`: never falling along the tokens: clip 0, then clip 1, then padding (2) at the end; every value occurs.
All inputs are finite; a program needn't handle non-finite values.
Results may differ from the reference program's by a relative error of at most 0.0003.
Values may be sent and summed in bfloat16 or wider, within the bound.
No kernel may reach another device: no remote copies, remote signals or barrier semaphores. Data moves between devices by JAX's collectives and lax.ppermute only.
A program may use at most 128 MiB of HBM per device.

```python
import jax
import jax.numpy as jnp
from jax import lax

HD = 128
SEQ = 16384


def draw_queries(key, part):
    key = jax.random.fold_in(key, 1)
    own = jax.random.normal(key, (SEQ, HD), jnp.float32)
    return own.astype(jnp.bfloat16)


def draw_keys(key, part):
    key = jax.random.fold_in(key, 2)
    own = jax.random.normal(key, (SEQ, HD), jnp.float32)
    return own.astype(jnp.bfloat16)


def draw_segment_ids(key, part):
    key = jax.random.fold_in(key, 5)
    first_key, second_key = jax.random.split(key)
    border = jax.random.randint(first_key, (), SEQ // 4, 3 * SEQ // 4 + 1)
    padding = jax.random.randint(second_key, (), 1, SEQ // 8 + 1)
    positions = jnp.arange(SEQ)
    return (positions >= border).astype(jnp.int32) + (positions >= SEQ - padding).astype(jnp.int32)


def block_scale(rng, dims, cuts, smallest, top_value):
    factor_of = 1.0
    for position, parts in cuts:
        steps = jax.random.uniform(jax.random.fold_in(jax.random.fold_in(rng, 6), position), (parts,), jnp.float32, smallest / len(cuts), top_value / len(cuts))
        factor_of = factor_of * jnp.repeat(jnp.exp(steps), dims[position] // parts).reshape((-1,) + (1,) * (len(dims) - 1 - position))
    return factor_of


def gaussian(rng, extent, spread, bound, pieces=(), held_as=jnp.bfloat16):
    level = block_scale(rng, extent, pieces, -0.22, 0.18) if pieces else 1.0
    drawn = jax.random.normal(rng, extent, jnp.float32) * spread * level
    return jnp.minimum(jnp.maximum(drawn, -bound), bound).astype(held_as)


def setup_inputs(seed: int = 0, part: int = 0) -> dict:
    splits = jax.random.split(jax.random.key(seed), 8)
    part_splits = jax.random.split(jax.random.fold_in(splits[7], part), 8)
    queries = draw_queries(jax.random.fold_in(jax.random.fold_in(splits[7], part), 71), part)
    keys = draw_keys(jax.random.fold_in(jax.random.fold_in(splits[7], part), 71), part)
    values = gaussian(part_splits[2], (SEQ, HD), 1.0, 6.0, ((0, 64),))
    tan_queries = gaussian(part_splits[3], (SEQ, HD), 1.0, 6.0, ((0, 64),))
    tan_keys = gaussian(part_splits[4], (SEQ, HD), 1.0, 6.0, ((0, 64),))
    tan_values = gaussian(part_splits[5], (SEQ, HD), 1.0, 6.0, ((0, 64),))
    segment_ids = draw_segment_ids(jax.random.fold_in(jax.random.fold_in(splits[7], part), 71), part)
    return {"queries": queries, "keys": keys, "values": values, "tan_queries": tan_queries, "tan_keys": tan_keys, "tan_values": tan_values, "segment_ids": segment_ids}


def reference(queries, keys, values, tan_queries, tan_keys, tan_values, segment_ids):
    scale = HD ** -0.5
    key_valid = segment_ids < 2
    block_rows = min(512, SEQ)
    count = SEQ // block_rows
    values_wide = values.astype(jnp.float32)
    tan_values_wide = tan_values.astype(jnp.float32)
    highest = lax.Precision.HIGHEST

    def one_block(args):
        query, tan_query, query_ids = args
        scores = jnp.dot(query, keys.T, preferred_element_type=jnp.float32) * scale
        tan_scores = (jnp.dot(tan_query, keys.T, preferred_element_type=jnp.float32)
                      + jnp.dot(query, tan_keys.T, preferred_element_type=jnp.float32)) * scale
        allowed = (query_ids[:, None] == segment_ids[None, :]) & key_valid[None, :]
        row_max = jnp.max(jnp.where(allowed, scores, jnp.float32(-1e30)), axis=1)
        weights = jnp.where(allowed, jnp.exp(scores - row_max[:, None]), jnp.float32(0.0))
        tilted = weights * tan_scores
        total = jnp.sum(weights, axis=1)
        tilt = jnp.sum(tilted, axis=1)
        plain = jnp.dot(weights, values_wide, precision=highest, preferred_element_type=jnp.float32)
        bent = (jnp.dot(tilted, values_wide, precision=highest, preferred_element_type=jnp.float32)
                + jnp.dot(weights, tan_values_wide, precision=highest, preferred_element_type=jnp.float32))
        valid = query_ids < 2
        denom = jnp.where(valid, total, jnp.float32(1.0))
        result = plain / denom[:, None]
        mean_tilt = tilt / denom
        tan_result = bent / denom[:, None] - mean_tilt[:, None] * result
        result = jnp.where(valid[:, None], result, jnp.float32(0.0))
        tan_result = jnp.where(valid[:, None], tan_result, jnp.float32(0.0))
        return result, tan_result

    attended, tan_attended = lax.map(one_block, (queries.reshape(count, block_rows, HD),
                                                 tan_queries.reshape(count, block_rows, HD),
                                                 segment_ids.reshape(count, block_rows)))
    return attended.reshape(SEQ, HD), tan_attended.reshape(SEQ, HD)
```

```python
import functools

import jax
import jax.numpy as jnp
import numpy as np
from jax import lax
from jax.experimental import pallas as pl
from jax.experimental.pallas import tpu as pltpu
from jax.sharding import Mesh, PartitionSpec as P

F32, BF16, I16 = jnp.float32, jnp.bfloat16, jnp.int16
AXES = ("z", "y", "x", "core")
SIZES = (2, 4, 4, 2)
ROWS = 256
WIDTH = 128
META = 16
KV_ROWS = 2 * ROWS + META
Q_ROWS = ROWS + META
SCALE = WIDTH**-0.5
LOG2E = 1.4426950408889634
BARRED = -(2.0**100)
FULL = 32767.0
VMEM = pl.BlockSpec(memory_space=pltpu.VMEM)
PARAMS = pltpu.CompilerParams(vmem_limit_bytes=48 * 2**20)


def times(left, right):
    return lax.dot_general(left, right, (((1,), (0,)), ((), ())), preferred_element_type=F32)


def turned(block):
    return block.astype(F32).T.astype(BF16)


def pack_kernel(q, k, v, tq, tk, tv, ids, kv_out, q_out):
    kv_out[0:ROWS, 0:WIDTH] = k[...]
    kv_out[0:ROWS, WIDTH : 2 * WIDTH] = tk[...]
    kv_out[ROWS : ROWS + WIDTH, :] = turned(v[...])
    kv_out[ROWS + WIDTH : 2 * ROWS, :] = turned(tv[...])
    q_out[0:WIDTH, :] = turned(tq[...])
    q_out[WIDTH : 2 * WIDTH, :] = turned(q[...])
    clip = ids[...]
    zeros = jnp.sum((clip == 0).astype(F32), axis=1, keepdims=True)
    ones = jnp.sum((clip == 1).astype(F32), axis=1, keepdims=True)
    row = lax.broadcasted_iota(jnp.int32, (META, ROWS), 0)
    meta = jnp.where(row == 0, zeros, jnp.where(row == 1, ones, 0.0)).astype(BF16)
    kv_out[2 * ROWS :, :] = meta
    q_out[ROWS:, :] = meta


def pack(q, k, v, tq, tk, tv, ids):
    return pl.pallas_call(
        pack_kernel,
        out_shape=(
            jax.ShapeDtypeStruct((KV_ROWS, ROWS), BF16),
            jax.ShapeDtypeStruct((Q_ROWS, ROWS), BF16),
        ),
        in_specs=[VMEM] * 7,
        out_specs=(VMEM, VMEM),
        name="pack",
    )(q, k, v, tq, tk, tv, ids.reshape(1, ROWS))


def split(wide):
    high = wide.astype(BF16)
    return high, (wide - high.astype(F32)).astype(BF16)


def fold(wide, op):
    return op(wide.reshape(wide.shape[0] // 8, 8, wide.shape[1]), axis=0)


def key_marks(meta):
    zeros, ones = meta[0:1, 0:WIDTH], meta[1:2, 0:WIDTH]
    row = lax.broadcasted_iota(jnp.int32, (ROWS, WIDTH), 0).astype(F32)
    lane = lax.broadcasted_iota(jnp.int32, (ROWS, WIDTH), 1)
    first = row < zeros
    second = (row >= zeros) & (row < zeros + ones)
    open_ = ((lane == 0) & first) | ((lane == 1) & second) | (lane > 2)
    return jnp.where(open_, 0.0, BARRED).astype(BF16)


def query_marks(meta):
    zeros, ones = meta[0:1, :], meta[1:2, :]
    row = lax.broadcasted_iota(jnp.int32, (WIDTH, ROWS), 0)
    lane = lax.broadcasted_iota(jnp.int32, (WIDTH, ROWS), 1).astype(F32)
    clip = jnp.where(lane < zeros, 0, jnp.where(lane < zeros + ones, 1, 2))
    return jnp.where(row == clip, 1.0, 0.0).astype(BF16)


def coded(value, levels):
    size = jnp.maximum(jnp.abs(value), 1e-30)
    exponent = jnp.ceil(jnp.log2(size)) + 1.0
    left = value * jnp.exp2(-exponent) * FULL
    rows = [exponent]
    for _ in range(levels):
        digit = jnp.round(left)
        rows.append(digit)
        left = (left - digit) * FULL
    return rows


def decoded(rows):
    exponent, digits = rows[0], rows[1:]
    value = digits[-1] * (1.0 / FULL)
    for digit in digits[-2::-1]:
        value = (value + digit) * (1.0 / FULL)
    return value * jnp.exp2(exponent)


def attend_kernel(pair, span, q_ref, *refs):
    kv, (out_ref, marked, scores) = refs[:-3], refs[-3:]
    blocks = len(kv)
    metas = [block[2 * ROWS :, :].astype(F32) for block in kv]
    key_count = functools.reduce(jnp.add, metas)
    for j, block in enumerate(kv):
        marked[j * ROWS : (j + 1) * ROWS, 0:WIDTH] = block[0:ROWS, 0:WIDTH]
        marked[j * ROWS : (j + 1) * ROWS, WIDTH:] = key_marks(metas[j])

    def one(i, carry):
        q_meta = q_ref[i, ROWS:, :].astype(F32)
        both = jnp.max((key_count * q_meta)[0:2, :])

        @pl.when(both > 0)
        def _():
            turned_q = q_ref[i, WIDTH : 2 * WIDTH, :]
            q_marked = jnp.concatenate([turned_q, query_marks(q_meta)], axis=0)
            q_both = q_ref[i, 0:ROWS, :]
            top = None
            for j in range(0, blocks, span):
                part = slice(j * ROWS, (j + span) * ROWS)
                own = times(marked[part], q_marked)
                scores[part] = own
                own_top = fold(own, jnp.max)
                top = own_top if top is None else jnp.maximum(top, own_top)
            top = jnp.max(top, axis=0, keepdims=True)
            total = jnp.zeros((8, ROWS), F32)
            tilt = jnp.zeros((8, ROWS), F32)
            plain = jnp.zeros((ROWS, ROWS), F32)
            bent = jnp.zeros((WIDTH, ROWS), F32)
            for j in range(0, blocks, span):
                part = slice(j * ROWS, (j + span) * ROWS)
                group = kv[j : j + span]
                tan_scores = times(jnp.concatenate([b[0:ROWS, :] for b in group], axis=0), q_both)
                weights = jnp.exp2((scores[part] - top) * (SCALE * LOG2E))
                tilted = weights * tan_scores
                total += fold(weights, jnp.sum)
                tilt += fold(tilted, jnp.sum)
                values = jnp.concatenate([b[ROWS : 2 * ROWS, :] for b in group], axis=1)
                high, low = split(weights)
                plain += times(values, high) + times(values, low)
                high, low = split(tilted)
                bent += times(values[0:WIDTH], high) + times(values[0:WIDTH], low)
            total = jnp.sum(total, axis=0, keepdims=True)
            tilt = jnp.sum(tilt, axis=0, keepdims=True) * SCALE
            share = 1.0 / total
            mean_tilt = tilt * share
            mean = plain[0:WIDTH] * share
            tan_mean = (bent * SCALE + plain[WIDTH:]) * share - mean_tilt * mean
            log_top = top * (SCALE * LOG2E)
            whole_top = jnp.maximum(jnp.ceil(log_top), -32768.0)
            weight = total * jnp.exp2(jnp.maximum(log_top - whole_top, -1.0))
            stats = [whole_top] + coded(weight, 2) + coded(mean_tilt, 2)
            for at, block in ((0, mean), (WIDTH, tan_mean)):
                code = coded(jnp.max(jnp.abs(block), axis=0, keepdims=True) * 1.0001, 1)
                stats += code
                step = FULL / jnp.maximum(decoded(code), 1e-30)
                out_ref[i, at : at + WIDTH, :] = jnp.round(block * step).astype(jnp.int32).astype(I16)
            stats += [jnp.zeros((1, ROWS), F32)] * (META - len(stats))
            out_ref[i, ROWS:, :] = jnp.concatenate(stats, axis=0).astype(jnp.int32).astype(I16)

        @pl.when(both <= 0)
        def _():
            row = lax.broadcasted_iota(jnp.int32, (META, ROWS), 0)
            out_ref[i, 0:ROWS, :] = jnp.zeros((ROWS, ROWS), I16)
            out_ref[i, ROWS:, :] = jnp.where(row == 0, -32768, 0).astype(I16)

        return carry

    lax.fori_loop(0, pair, one, 0)


def attend(queries, kv):
    pair = queries.shape[0]
    return pl.pallas_call(
        functools.partial(attend_kernel, pair, 2),
        out_shape=jax.ShapeDtypeStruct((pair, Q_ROWS, ROWS), I16),
        in_specs=[VMEM] * (1 + len(kv)),
        out_specs=VMEM,
        scratch_shapes=[
            pltpu.VMEM((len(kv) * ROWS, 2 * WIDTH), BF16),
            pltpu.VMEM((len(kv) * ROWS, ROWS), F32),
        ],
        compiler_params=PARAMS,
        name="attend",
    )(queries, *kv)


def combine_kernel(ids_ref, *refs):
    parts, (out_ref, tan_ref) = refs[:-2], refs[-2:]
    half = len(parts) // 2
    found = []
    for n, part in enumerate(parts):
        side = 0 if n < half else 1
        stats = part[side, ROWS:, :].astype(jnp.int32).astype(F32)
        rows = [stats[r : r + 1, :] for r in range(11)]
        found.append(
            (part, side, rows[0], decoded(rows[1:4]), decoded(rows[4:7]), decoded(rows[7:9]), decoded(rows[9:11]))
        )
    top = functools.reduce(jnp.maximum, [f[2] for f in found])
    weights = [f[3] * jnp.exp2(f[2] - top) for f in found]
    total = functools.reduce(jnp.add, weights)
    share = 1.0 / jnp.where(total > 0, total, 1.0)
    weights = [w * share for w in weights]
    mean_tilt = functools.reduce(jnp.add, [w * f[4] for w, f in zip(weights, found)])
    result = jnp.zeros((WIDTH, ROWS), F32)
    tan_result = jnp.zeros((WIDTH, ROWS), F32)
    for weight, (part, side, _, _, tilt, size, tan_size) in zip(weights, found):
        mean = part[side, 0:WIDTH, :].astype(jnp.int32).astype(F32) * (size * (1.0 / FULL))
        tan_mean = part[side, WIDTH : 2 * WIDTH, :].astype(jnp.int32).astype(F32) * (tan_size * (1.0 / FULL))
        result += weight * mean
        tan_result += weight * tan_mean + (weight * (tilt - mean_tilt)) * mean
    valid = ids_ref[...] < 2
    out_ref[...] = jnp.where(valid, result, 0.0).T
    tan_ref[...] = jnp.where(valid, tan_result, 0.0).T


def combine(ids, parts):
    shape = jax.ShapeDtypeStruct((ROWS, WIDTH), F32)
    return pl.pallas_call(
        combine_kernel,
        out_shape=(shape, shape),
        in_specs=[VMEM] * (1 + len(parts)),
        out_specs=(VMEM, VMEM),
        compiler_params=PARAMS,
        name="combine",
    )(ids.reshape(1, ROWS), *parts)


def pairs_of(move):
    return [
        (i, int(np.ravel_multi_index(move(*np.unravel_index(i, SIZES)), SIZES))) for i in range(int(np.prod(SIZES)))
    ]


def across_x(shift):
    return pairs_of(lambda z, y, x, c: (z, y, (x + shift) % 4, c))


SIBLING = pairs_of(lambda z, y, x, c: (z, y, x, 1 - c))


def query_route(slot):
    along_z, along_y = slot // 2, 2 * (slot % 2)
    return pairs_of(lambda z, y, x, c: ((z + along_z) % 2, (y + along_y + c) % 4, x, y % 2))


def per_device(queries, keys, values, tan_queries, tan_keys, tan_values, segment_ids):
    move = functools.partial(lax.ppermute, axis_name=AXES)
    kv, q = pack(queries, keys, values, tan_queries, tan_keys, tan_values, segment_ids)
    q_pair = jnp.stack([q, move(q, perm=SIBLING)])
    mine = [kv] + [move(kv, perm=across_x(shift)) for shift in (1, 3, 2)]
    all_kv = mine + [move(block, perm=SIBLING) for block in mine]
    parts = []
    for slot in (3, 2, 1, 0):
        route = query_route(slot)
        visiting = move(q_pair, perm=route)
        found = attend(visiting, all_kv)
        parts.append(move(found, perm=[(b, a) for a, b in route]))
    parts += [move(part, perm=SIBLING) for part in parts]
    return combine(segment_ids, parts)


def solution(mesh):
    fine = Mesh(mesh.devices.reshape(SIZES + (2,)), AXES + ("batch",))
    rows = P(("batch",) + AXES)
    table = P(("batch",) + AXES, None)
    return jax.shard_map(
        per_device,
        mesh=fine,
        in_specs=(table,) * 6 + (rows,),
        out_specs=(table, table),
        check_vma=False,
    )
```

```python
import functools

import jax
import jax.numpy as jnp
import numpy as np
from jax import lax
from jax.experimental import pallas as pl
from jax.experimental.pallas import tpu as pltpu
from jax.sharding import Mesh, PartitionSpec as P

F32, BF16, I16 = jnp.float32, jnp.bfloat16, jnp.int16
AXES = ("z", "y", "x", "core")
SIZES = (2, 4, 4, 2)
ROWS = 256
WIDTH = 128
META = 16
KV_ROWS = 2 * ROWS + META
Q_ROWS = ROWS + META
SCALE = WIDTH**-0.5
LOG2E = 1.4426950408889634
BARRED = -(2.0**100)
UNSEEN = -(2.0**120)
STATE_ROWS = 408
FULL = 32767.0
VMEM = pl.BlockSpec(memory_space=pltpu.VMEM)
WAITED = pl.CostEstimate(flops=2 * 10**9, bytes_accessed=1, transcendentals=0)
LIGHT = pl.CostEstimate(flops=1, bytes_accessed=1, transcendentals=0)
SMALL = pltpu.CompilerParams(vmem_limit_bytes=8 * 2**20)
LARGE = pltpu.CompilerParams(vmem_limit_bytes=16 * 2**20)


def times(left, right):
    return lax.dot_general(left, right, (((1,), (0,)), ((), ())), preferred_element_type=F32)


def turned(block):
    return block.astype(F32).T.astype(BF16)


def pack_kernel(*refs):
    sources, (kv_out, q_out), held, done = refs[:7], refs[7:9], refs[9:16], refs[16]
    copies = [pltpu.make_async_copy(a, b, done.at[n]) for n, (a, b) in enumerate(zip(sources, held))]
    for copy in copies:
        copy.start()
    for copy in copies:
        copy.wait()
    q, k, v, tq, tk, tv, ids = held
    kv_out[0:ROWS, 0:WIDTH] = k[...]
    kv_out[0:ROWS, WIDTH : 2 * WIDTH] = tk[...]
    kv_out[ROWS : ROWS + WIDTH, :] = turned(v[...])
    kv_out[ROWS + WIDTH : 2 * ROWS, :] = turned(tv[...])
    q_out[0:WIDTH, :] = turned(tq[...])
    q_out[WIDTH : 2 * WIDTH, :] = turned(q[...])
    clip = ids[...]
    zeros = jnp.sum((clip == 0).astype(F32), axis=1, keepdims=True)
    ones = jnp.sum((clip == 1).astype(F32), axis=1, keepdims=True)
    row = lax.broadcasted_iota(jnp.int32, (META, ROWS), 0)
    meta = jnp.where(row == 0, zeros, jnp.where(row == 1, ones, 0.0)).astype(BF16)
    kv_out[2 * ROWS :, :] = meta
    q_out[ROWS:, :] = meta


def pack(q, k, v, tq, tk, tv, ids):
    return pl.pallas_call(
        pack_kernel,
        out_shape=(
            jax.ShapeDtypeStruct((KV_ROWS, ROWS), BF16),
            jax.ShapeDtypeStruct((Q_ROWS, ROWS), BF16),
        ),
        in_specs=[pl.BlockSpec(memory_space=pl.ANY)] * 7,
        out_specs=(VMEM, VMEM),
        scratch_shapes=[pltpu.VMEM((ROWS, WIDTH), BF16)] * 6
        + [pltpu.VMEM((1, ROWS), jnp.int32), pltpu.SemaphoreType.DMA((7,))],
        compiler_params=SMALL,
        cost_estimate=LIGHT,
        name="pack",
    )(*[pltpu.with_memory_space_constraint(a, pltpu.HBM) for a in (q, k, v, tq, tk, tv, ids.reshape(1, ROWS))])


def split(wide):
    high = wide.astype(BF16)
    return high, (wide - high.astype(F32)).astype(BF16)


def fold(wide, op):
    return op(wide.reshape(wide.shape[0] // 8, 8, wide.shape[1]), axis=0)


def key_marks(meta):
    zeros, ones = meta[0:1, 0:WIDTH], meta[1:2, 0:WIDTH]
    row = lax.broadcasted_iota(jnp.int32, (ROWS, WIDTH), 0).astype(F32)
    lane = lax.broadcasted_iota(jnp.int32, (ROWS, WIDTH), 1)
    first = row < zeros
    second = (row >= zeros) & (row < zeros + ones)
    open_ = ((lane == 0) & first) | ((lane == 1) & second) | (lane > 2)
    return jnp.where(open_, 0.0, BARRED).astype(BF16)


def query_marks(meta):
    zeros, ones = meta[0:1, :], meta[1:2, :]
    row = lax.broadcasted_iota(jnp.int32, (WIDTH, ROWS), 0)
    lane = lax.broadcasted_iota(jnp.int32, (WIDTH, ROWS), 1).astype(F32)
    clip = jnp.where(lane < zeros, 0, jnp.where(lane < zeros + ones, 1, 2))
    return jnp.where(row == clip, 1.0, 0.0).astype(BF16)


def coded(value, levels):
    size = jnp.maximum(jnp.abs(value), 1e-30)
    exponent = jnp.ceil(jnp.log2(size)) + 1.0
    left = value * jnp.exp2(-exponent) * FULL
    rows = [exponent]
    for _ in range(levels):
        digit = jnp.round(left)
        rows.append(digit)
        left = (left - digit) * FULL
    return rows


def decoded(rows):
    exponent, digits = rows[0], rows[1:]
    value = digits[-1] * (1.0 / FULL)
    for digit in digits[-2::-1]:
        value = (value + digit) * (1.0 / FULL)
    return value * jnp.exp2(exponent)


def blocks_of(refs):
    return [ref.at[n] for ref in refs for n in range(ref.shape[0])]


def choose_kernel(core, *refs):
    half = (len(refs) - 1) // 2
    for side in range(2):

        @pl.when(core[0] == side)
        def _(side=side):
            for n, block in enumerate(refs[side * half : (side + 1) * half]):
                refs[-1][n] = block[0]


def choose(core, first, second):
    return pl.pallas_call(
        choose_kernel,
        out_shape=jax.ShapeDtypeStruct((len(first),) + first[0].shape[1:], first[0].dtype),
        in_specs=[pl.BlockSpec(memory_space=pltpu.SMEM)] + [VMEM] * 2 * len(first),
        out_specs=VMEM,
        compiler_params=SMALL,
        cost_estimate=LIGHT,
        name="choose",
    )(core, *first, *second)


def stack_kernel(counts, *refs):
    at = 0
    for count, group in zip(counts, refs[:-1]):
        refs[-1][at : at + count] = group[0:count]
        at += count


def stack(*groups, counts):
    return pl.pallas_call(
        functools.partial(stack_kernel, counts),
        out_shape=jax.ShapeDtypeStruct((sum(counts),) + groups[0].shape[1:], groups[0].dtype),
        in_specs=[VMEM] * len(groups),
        out_specs=VMEM,
        compiler_params=SMALL,
        cost_estimate=LIGHT,
        name="stack",
    )(*groups)


def gather_kernel(*refs):
    blocks, kv, marked = blocks_of(refs[:-2]), refs[-2], refs[-1]
    for n, block in enumerate(blocks):
        kv[n] = block[...]
        rows = slice(n * ROWS, (n + 1) * ROWS)
        marked[rows, 0:WIDTH] = block[0:ROWS, 0:WIDTH]
        marked[rows, WIDTH:] = key_marks(block[2 * ROWS :, :].astype(F32))


def gather(*groups):
    blocks = sum(group.shape[0] for group in groups)
    return pl.pallas_call(
        gather_kernel,
        out_shape=(
            jax.ShapeDtypeStruct((blocks, KV_ROWS, ROWS), BF16),
            jax.ShapeDtypeStruct((blocks * ROWS, 2 * WIDTH), BF16),
        ),
        in_specs=[VMEM] * len(groups),
        out_specs=(VMEM, VMEM),
        compiler_params=SMALL,
        cost_estimate=LIGHT,
        name="gather",
    )(*groups)


def visit(q_block, kv, marked, scores, state, span):
    blocks = len(kv)
    q_marked = jnp.concatenate(
        [q_block[WIDTH : 2 * WIDTH, :], query_marks(q_block[ROWS:, :].astype(F32))], axis=0
    )
    q_both = q_block[0:ROWS, :]
    top = None
    for j in range(0, blocks, span):
        part = slice(j * ROWS, (j + span) * ROWS)
        own = times(marked[part], q_marked)
        scores[part] = own
        own_top = fold(own, jnp.max)
        top = own_top if top is None else jnp.maximum(top, own_top)
    top = jnp.max(top, axis=0, keepdims=True)
    if state is None:
        total = jnp.zeros((8, ROWS), F32)
        tilt = jnp.zeros((8, ROWS), F32)
        plain = jnp.zeros((ROWS, ROWS), F32)
        bent = jnp.zeros((WIDTH, ROWS), F32)
    else:
        total, tilt, old_top, plain, bent = state
        top = jnp.maximum(top, old_top)
        less = jnp.exp2((old_top - top) * (SCALE * LOG2E))
        total, tilt, plain, bent = total * less, tilt * less, plain * less, bent * less
    for j in range(0, blocks, span):
        part = slice(j * ROWS, (j + span) * ROWS)
        group = kv[j : j + span]
        tan_scores = times(jnp.concatenate([b[0:ROWS, :] for b in group], axis=0), q_both)
        weights = jnp.exp2((scores[part] - top) * (SCALE * LOG2E))
        tilted = weights * tan_scores
        total += fold(weights, jnp.sum)
        tilt += fold(tilted, jnp.sum)
        values = jnp.concatenate([b[ROWS : 2 * ROWS, :] for b in group], axis=1)
        high, low = split(weights)
        plain += times(values, high) + times(values, low)
        high, low = split(tilted)
        bent += times(values[0:WIDTH], high) + times(values[0:WIDTH], low)
    return total, tilt, top, plain, bent


def load_state(ref):
    return ref[384:392, :], ref[392:400, :], ref[400:401, :], ref[0:ROWS, :], ref[ROWS:384, :]


def store_state(ref, state):
    total, tilt, top, plain, bent = state
    ref[384:392, :] = total
    ref[392:400, :] = tilt
    ref[400:408, :] = jnp.broadcast_to(top, (8, ROWS))
    ref[0:ROWS, :] = plain
    ref[ROWS:384, :] = bent


def clips_met(kv, q_block):
    count = functools.reduce(jnp.add, [block[2 * ROWS :, :].astype(F32) for block in kv])
    return jnp.max((count * q_block[ROWS:, :].astype(F32))[0:2, :])


def begin_kernel(groups, span, queries, *refs):
    kv, marked, state, scores = blocks_of(refs[:groups]), refs[-3], refs[-2], refs[-1]

    def one(i, carry):
        met = clips_met(kv, queries.at[i])

        @pl.when(met > 0)
        def _():
            store_state(state.at[i], visit(queries.at[i], kv, marked, scores, None, span))

        @pl.when(met <= 0)
        def _():
            state[i] = jnp.zeros((STATE_ROWS, ROWS), F32)
            state[i, 400:408, :] = jnp.full((8, ROWS), UNSEEN, F32)

        return carry

    lax.fori_loop(0, queries.shape[0], one, 0)


def go_on_kernel(groups, span, queries, *refs):
    kv, marked, state, out, scores = blocks_of(refs[:groups]), refs[-4], refs[-3], refs[-2], refs[-1]

    def one(i, carry):
        met = clips_met(kv, queries.at[i])

        @pl.when(met > 0)
        def _():
            store_state(out.at[i], visit(queries.at[i], kv, marked, scores, load_state(state.at[i]), span))

        @pl.when(met <= 0)
        def _():
            out[i] = state[i]

        return carry

    lax.fori_loop(0, queries.shape[0], one, 0)


def end_kernel(first, groups, span, queries, *refs):
    kv, marked, state, out, last, scores = blocks_of(refs[:groups]), refs[-5], refs[-4], refs[-3], refs[-2], refs[-1]

    def one(i, carry):
        met = clips_met(kv, queries.at[first + i])

        @pl.when(met > 0)
        def _():
            store_state(last, visit(queries.at[first + i], kv, marked, scores, load_state(state.at[first + i]), span))

        @pl.when(met <= 0)
        def _():
            last[...] = state[first + i]

        total, tilt, top, plain, bent = load_state(last)
        total = jnp.sum(total, axis=0, keepdims=True)
        tilt = jnp.sum(tilt, axis=0, keepdims=True) * SCALE
        share = 1.0 / jnp.where(total > 0, total, 1.0)
        mean_tilt = tilt * share
        mean = plain[0:WIDTH] * share
        tan_mean = (bent * SCALE + plain[WIDTH:]) * share - mean_tilt * mean
        log_top = top * (SCALE * LOG2E)
        whole_top = jnp.maximum(jnp.ceil(log_top), -32768.0)
        weight = total * jnp.exp2(jnp.maximum(log_top - whole_top, -1.0))
        stats = [whole_top] + coded(weight, 2) + coded(mean_tilt, 2)
        for at, block in ((0, mean), (WIDTH, tan_mean)):
            code = coded(jnp.max(jnp.abs(block), axis=0, keepdims=True) * 1.0001, 1)
            stats += code
            step = FULL / jnp.maximum(decoded(code), 1e-30)
            out[i, at : at + WIDTH, :] = jnp.round(block * step).astype(jnp.int32).astype(I16)
        stats += [jnp.zeros((1, ROWS), F32)] * (META - len(stats))
        out[i, ROWS:, :] = jnp.concatenate(stats, axis=0).astype(jnp.int32).astype(I16)
        return carry

    lax.fori_loop(0, out.shape[0], one, 0)


def attend(queries, gathered, state=None, which=None, expect=LIGHT):
    groups, marked = gathered[:-1], gathered[-1]
    blocks = sum(group.shape[0] for group in groups)
    keys, span = blocks * ROWS, blocks // 2
    scores = pltpu.VMEM((keys, ROWS), F32)
    out_shape = jax.ShapeDtypeStruct((queries.shape[0], STATE_ROWS, ROWS), F32)
    operands, scratch, count = [queries, *groups, marked], [scores], queries.shape[0]
    if state is None:
        kernel = functools.partial(begin_kernel, len(groups), span)
    else:
        operands.append(state)
        kernel = functools.partial(go_on_kernel, len(groups), span)
    if which is not None:
        first, count = which
        kernel = functools.partial(end_kernel, first, len(groups), span)
        out_shape = jax.ShapeDtypeStruct((count, Q_ROWS, ROWS), I16)
        scratch = [pltpu.VMEM((STATE_ROWS, ROWS), F32), scores]
    return pl.pallas_call(
        kernel,
        out_shape=out_shape,
        in_specs=[VMEM] * len(operands),
        out_specs=VMEM,
        scratch_shapes=scratch,
        compiler_params=LARGE,
        cost_estimate=expect,
        name="attend",
    )(*operands)


def combine_kernel(sides, ids_ref, *refs):
    parts, (out_ref, tan_ref) = refs[:-2], refs[-2:]
    found = []
    for part in [part.at[side] for part, side in zip(parts, sides)]:
        stats = part[ROWS:, :].astype(jnp.int32).astype(F32)
        rows = [stats[r : r + 1, :] for r in range(11)]
        found.append(
            (part, rows[0], decoded(rows[1:4]), decoded(rows[4:7]), decoded(rows[7:9]), decoded(rows[9:11]))
        )
    top = functools.reduce(jnp.maximum, [f[1] for f in found])
    weights = [f[2] * jnp.exp2(f[1] - top) for f in found]
    total = functools.reduce(jnp.add, weights)
    share = 1.0 / jnp.where(total > 0, total, 1.0)
    weights = [w * share for w in weights]
    mean_tilt = functools.reduce(jnp.add, [w * f[3] for w, f in zip(weights, found)])
    result = jnp.zeros((WIDTH, ROWS), F32)
    tan_result = jnp.zeros((WIDTH, ROWS), F32)
    for weight, (part, _, _, tilt, size, tan_size) in zip(weights, found):
        mean = part[0:WIDTH, :].astype(jnp.int32).astype(F32) * (size * (1.0 / FULL))
        tan_mean = part[WIDTH : 2 * WIDTH, :].astype(jnp.int32).astype(F32) * (tan_size * (1.0 / FULL))
        result += weight * mean
        tan_result += weight * tan_mean + (weight * (tilt - mean_tilt)) * mean
    valid = ids_ref[...] < 2
    out_ref[...] = jnp.where(valid, result, 0.0).T
    tan_ref[...] = jnp.where(valid, tan_result, 0.0).T


def combine(ids, parts, sides):
    shape = jax.ShapeDtypeStruct((ROWS, WIDTH), F32)
    return pl.pallas_call(
        functools.partial(combine_kernel, sides),
        out_shape=(shape, shape),
        in_specs=[VMEM] * (1 + len(parts)),
        out_specs=(VMEM, VMEM),
        compiler_params=SMALL,
        cost_estimate=LIGHT,
        name="combine",
    )(ids.reshape(1, ROWS), *parts)


def pairs_of(move):
    return [
        (i, int(np.ravel_multi_index(move(*np.unravel_index(i, SIZES)), SIZES))) for i in range(int(np.prod(SIZES)))
    ]


def route(first, second):
    return pairs_of(lambda z, y, x, c: (second if c else first)(z, y, x) + (c,))


SIBLING = pairs_of(lambda z, y, x, c: (z, y, x, 1 - c))
RIGHT = route(*[lambda z, y, x: (z, y, (x + 1) % 4)] * 2)
LEFT = route(*[lambda z, y, x: (z, y, (x + 3) % 4)] * 2)
BOTH_WAYS = route(lambda z, y, x: (z, y, (x + 1) % 4), lambda z, y, x: (z, y, (x + 3) % 4))
LEVEL = route(*[lambda z, y, x: (z, y ^ 1, x)] * 2)
Q_Z = route(*[lambda z, y, x: (1 - z, y, x)] * 2)
Q_Y = route(*[lambda z, y, x: (z, (y + 2) % 4, x)] * 2)
Q_FAR = route(*[lambda z, y, x: (1 - z, (y + 2) % 4, x)] * 2)


def back(pairs):
    return [(b, a) for a, b in pairs]


def together(*arrays):
    return lax.optimization_barrier(arrays)


def per_device(queries, keys, values, tan_queries, tan_keys, tan_values, segment_ids):
    move = functools.partial(lax.ppermute, axis_name=AXES)

    def sibling(group):
        return move(group, perm=SIBLING)

    def both(group):
        return [group, sibling(group)]

    core = lax.axis_index("core").reshape(1)
    kv, q = pack(queries, keys, values, tan_queries, tan_keys, tan_values, segment_ids)
    kv, q = kv[None], q[None]
    level = move(kv, perm=LEVEL)
    right, left = move(kv, perm=RIGHT), move(kv, perm=LEFT)
    q_z, q_y = move(q, perm=Q_Z), move(q, perm=Q_Y)
    level, right, left, q_z = together(level, right, left, q_z)
    level_right, level_left = move(level, perm=RIGHT), move(level, perm=LEFT)
    first = gather(*both(kv), *both(level), *both(right), *both(left))
    held = stack(q_z, q, counts=(1, 1))
    state = attend(held, first)

    level_right, level_left, q_y, state = together(level_right, level_left, q_y, state)
    on = move(choose(core, (right, level_right), (left, level_left)), perm=BOTH_WAYS)
    q_far = move(q_y, perm=Q_Z)
    more = both(level_right) + both(level_left)
    y_state = attend(q_y, first, expect=WAITED)
    *more, y_state = together(*more, y_state)
    second = gather(*more)
    state = attend(held, second, state)
    y_state = attend(q_y, second, y_state)

    on, q_far, state, y_state = together(on, q_far, state, y_state)
    on_other = sibling(on)
    far_state = attend(q_far, second, attend(q_far, first, expect=WAITED), expect=WAITED)
    on_other, far_state = together(on_other, far_state)
    third = gather(on, on_other)
    out_far, y_state = together(attend(q_far, third, far_state, (0, 1)), y_state)
    out_y, state = together(attend(q_y, third, y_state, (0, 1)), state)
    out_z, state = together(attend(held, third, state, (0, 1)), state)
    back_z = move(out_z, perm=back(Q_Z))
    back_y = move(out_y, perm=back(Q_Y))
    back_far = move(out_far, perm=back(Q_FAR))
    back_far, state = together(back_far, state)
    mine = attend(held, third, state, (1, 1))
    return combine(segment_ids, together(mine, back_z, back_y, back_far), (0, 0, 0, 0))


def solution(mesh):
    fine = Mesh(mesh.devices.reshape(SIZES + (2,)), AXES + ("batch",))
    rows = P(("batch",) + AXES)
    table = P(("batch",) + AXES, None)
    return jax.shard_map(
        per_device,
        mesh=fine,
        in_specs=(table,) * 6 + (rows,),
        out_specs=(table, table),
        check_vma=False,
    )
```

```python
import functools

import jax
import jax.numpy as jnp
import numpy as np
from jax import lax
from jax.experimental import pallas as pl
from jax.experimental.pallas import tpu as pltpu
from jax.sharding import Mesh, PartitionSpec as P

F32, BF16, I16 = jnp.float32, jnp.bfloat16, jnp.int16
AXES = ("z", "y", "x", "core")
SIZES = (2, 4, 4, 2)
ROWS = 256
WIDTH = 128
META = 16
KV_ROWS = 2 * ROWS + META
Q_ROWS = ROWS + META
SCALE = WIDTH**-0.5
LOG2E = 1.4426950408889634
BARRED = -(2.0**100)
UNSEEN = -(2.0**120)
STATE_ROWS = 424
FULL = 32767.0
VMEM = pl.BlockSpec(memory_space=pltpu.VMEM)
WAITED = pl.CostEstimate(flops=2 * 10**9, bytes_accessed=1, transcendentals=0)
LIGHT = pl.CostEstimate(flops=1, bytes_accessed=1, transcendentals=0)
SMALL = pltpu.CompilerParams(vmem_limit_bytes=8 * 2**20)
LARGE = pltpu.CompilerParams(vmem_limit_bytes=16 * 2**20)


def times(left, right):
    return lax.dot_general(left, right, (((1,), (0,)), ((), ())), preferred_element_type=F32)


def turned(block):
    return block.astype(F32).T.astype(BF16)


def pack_kernel(*refs):
    sources, (kv_out, q_out), held, done = refs[:7], refs[7:9], refs[9:16], refs[16]
    copies = [pltpu.make_async_copy(a, b, done.at[n]) for n, (a, b) in enumerate(zip(sources, held))]
    for copy in copies:
        copy.start()
    for copy in copies:
        copy.wait()
    q, k, v, tq, tk, tv, ids = held
    kv_out[0:ROWS, 0:WIDTH] = k[...]
    kv_out[0:ROWS, WIDTH : 2 * WIDTH] = tk[...]
    kv_out[ROWS : ROWS + WIDTH, :] = turned(v[...])
    kv_out[ROWS + WIDTH : 2 * ROWS, :] = turned(tv[...])
    q_out[0:WIDTH, :] = turned(tq[...])
    q_out[WIDTH : 2 * WIDTH, :] = turned(q[...])
    clip = ids[...]
    zeros = jnp.sum((clip == 0).astype(F32), axis=1, keepdims=True)
    ones = jnp.sum((clip == 1).astype(F32), axis=1, keepdims=True)
    row = lax.broadcasted_iota(jnp.int32, (META, ROWS), 0)
    meta = jnp.where(row == 0, zeros, jnp.where(row == 1, ones, 0.0)).astype(BF16)
    kv_out[2 * ROWS :, :] = meta
    q_out[ROWS:, :] = meta


def pack(q, k, v, tq, tk, tv, ids):
    return pl.pallas_call(
        pack_kernel,
        out_shape=(
            jax.ShapeDtypeStruct((KV_ROWS, ROWS), BF16),
            jax.ShapeDtypeStruct((Q_ROWS, ROWS), BF16),
        ),
        in_specs=[pl.BlockSpec(memory_space=pl.ANY)] * 7,
        out_specs=(VMEM, VMEM),
        scratch_shapes=[pltpu.VMEM((ROWS, WIDTH), BF16)] * 6
        + [pltpu.VMEM((1, ROWS), jnp.int32), pltpu.SemaphoreType.DMA((7,))],
        compiler_params=SMALL,
        cost_estimate=LIGHT,
        name="pack",
    )(*[pltpu.with_memory_space_constraint(a, pltpu.HBM) for a in (q, k, v, tq, tk, tv, ids.reshape(1, ROWS))])


def split(wide):
    high = wide.astype(BF16)
    return high, (wide - high.astype(F32)).astype(BF16)


def fold(wide, op):
    return op(wide.reshape(wide.shape[0] // 8, 8, wide.shape[1]), axis=0)


def key_marks(meta):
    zeros, ones = meta[0:1, 0:WIDTH], meta[1:2, 0:WIDTH]
    row = lax.broadcasted_iota(jnp.int32, (ROWS, WIDTH), 0).astype(F32)
    lane = lax.broadcasted_iota(jnp.int32, (ROWS, WIDTH), 1)
    first = row < zeros
    second = (row >= zeros) & (row < zeros + ones)
    open_ = ((lane == 0) & first) | ((lane == 1) & second) | (lane > 2)
    return jnp.where(open_, 0.0, BARRED).astype(BF16)


def query_marks(meta):
    zeros, ones = meta[0:1, :], meta[1:2, :]
    row = lax.broadcasted_iota(jnp.int32, (WIDTH, ROWS), 0)
    lane = lax.broadcasted_iota(jnp.int32, (WIDTH, ROWS), 1).astype(F32)
    clip = jnp.where(lane < zeros, 0, jnp.where(lane < zeros + ones, 1, 2))
    return jnp.where(row == clip, 1.0, 0.0).astype(BF16)


def coded(value, levels):
    size = jnp.maximum(jnp.abs(value), 1e-30)
    exponent = jnp.ceil(jnp.log2(size)) + 1.0
    left = value * jnp.exp2(-exponent) * FULL
    rows = [exponent]
    for _ in range(levels):
        digit = jnp.round(left)
        rows.append(digit)
        left = (left - digit) * FULL
    return rows


def decoded(rows):
    exponent, digits = rows[0], rows[1:]
    value = digits[-1] * (1.0 / FULL)
    for digit in digits[-2::-1]:
        value = (value + digit) * (1.0 / FULL)
    return value * jnp.exp2(exponent)


def blocks_of(refs):
    return [ref.at[n] for ref in refs for n in range(ref.shape[0])]


def choose_kernel(core, *refs):
    half = (len(refs) - 1) // 2
    for side in range(2):

        @pl.when(core[0] == side)
        def _(side=side):
            for n, block in enumerate(refs[side * half : (side + 1) * half]):
                refs[-1][n] = block[0]


def choose(core, first, second):
    return pl.pallas_call(
        choose_kernel,
        out_shape=jax.ShapeDtypeStruct((len(first),) + first[0].shape[1:], first[0].dtype),
        in_specs=[pl.BlockSpec(memory_space=pltpu.SMEM)] + [VMEM] * 2 * len(first),
        out_specs=VMEM,
        compiler_params=SMALL,
        cost_estimate=LIGHT,
        name="choose",
    )(core, *first, *second)


def stack_kernel(counts, *refs):
    at = 0
    for count, group in zip(counts, refs[:-1]):
        refs[-1][at : at + count] = group[0:count]
        at += count


def stack(*groups, counts):
    return pl.pallas_call(
        functools.partial(stack_kernel, counts),
        out_shape=jax.ShapeDtypeStruct((sum(counts),) + groups[0].shape[1:], groups[0].dtype),
        in_specs=[VMEM] * len(groups),
        out_specs=VMEM,
        compiler_params=SMALL,
        cost_estimate=LIGHT,
        name="stack",
    )(*groups)


def gather_kernel(*refs):
    blocks, kv, marked = blocks_of(refs[:-2]), refs[-2], refs[-1]
    for n, block in enumerate(blocks):
        kv[n] = block[...]
        rows = slice(n * ROWS, (n + 1) * ROWS)
        marked[rows, 0:WIDTH] = block[0:ROWS, 0:WIDTH]
        marked[rows, WIDTH:] = key_marks(block[2 * ROWS :, :].astype(F32))


def gather(*groups):
    blocks = sum(group.shape[0] for group in groups)
    return pl.pallas_call(
        gather_kernel,
        out_shape=(
            jax.ShapeDtypeStruct((blocks, KV_ROWS, ROWS), BF16),
            jax.ShapeDtypeStruct((blocks * ROWS, 2 * WIDTH), BF16),
        ),
        in_specs=[VMEM] * len(groups),
        out_specs=(VMEM, VMEM),
        compiler_params=SMALL,
        cost_estimate=LIGHT,
        name="gather",
    )(*groups)


def visit(q_block, kv, marked, scores, state, span):
    blocks = len(kv)
    q_marked = jnp.concatenate(
        [q_block[WIDTH : 2 * WIDTH, :], query_marks(q_block[ROWS:, :].astype(F32))], axis=0
    )
    q_both = q_block[0:ROWS, :]
    top = None
    for j in range(0, blocks, span):
        part = slice(j * ROWS, (j + span) * ROWS)
        own = times(marked[part], q_marked)
        scores[part] = own
        own_top = fold(own, jnp.max)
        top = own_top if top is None else jnp.maximum(top, own_top)
    top = jnp.max(top, axis=0, keepdims=True)
    if state is None:
        plain = jnp.zeros((ROWS + META, ROWS), F32)
        bent = jnp.zeros((WIDTH + META, ROWS), F32)
    else:
        old_top, plain, bent = state
        top = jnp.maximum(top, old_top)
        less = jnp.exp2((old_top - top) * (SCALE * LOG2E))
        plain, bent = plain * less, bent * less
    ones = jnp.ones((META, span * ROWS), BF16)
    for j in range(0, blocks, span):
        part = slice(j * ROWS, (j + span) * ROWS)
        group = kv[j : j + span]
        tan_scores = times(jnp.concatenate([b[0:ROWS, :] for b in group], axis=0), q_both)
        weights = jnp.exp2((scores[part] - top) * (SCALE * LOG2E))
        tilted = weights * tan_scores
        values = jnp.concatenate([b[ROWS : 2 * ROWS, :] for b in group], axis=1)
        both = jnp.concatenate([values, ones], axis=0)
        one = jnp.concatenate([values[0:WIDTH], ones], axis=0)
        high, low = split(weights)
        plain += times(both, high) + times(both, low)
        high, low = split(tilted)
        bent += times(one, high) + times(one, low)
    return top, plain, bent


def load_state(ref):
    return ref[416:417, :], ref[0:272, :], ref[272:416, :]


def store_state(ref, state):
    top, plain, bent = state
    ref[0:272, :] = plain
    ref[272:416, :] = bent
    ref[416:424, :] = jnp.broadcast_to(top, (8, ROWS))


def clips_met(kv, q_block):
    count = functools.reduce(jnp.add, [block[2 * ROWS :, :].astype(F32) for block in kv])
    return jnp.max((count * q_block[ROWS:, :].astype(F32))[0:2, :])


def begin_kernel(groups, span, queries, *refs):
    kv, marked, state, scores = blocks_of(refs[:groups]), refs[-3], refs[-2], refs[-1]

    def one(i, carry):
        met = clips_met(kv, queries.at[i])

        @pl.when(met > 0)
        def _():
            store_state(state.at[i], visit(queries.at[i], kv, marked, scores, None, span))

        @pl.when(met <= 0)
        def _():
            state[i] = jnp.zeros((STATE_ROWS, ROWS), F32)
            state[i, 416:424, :] = jnp.full((8, ROWS), UNSEEN, F32)

        return carry

    lax.fori_loop(0, queries.shape[0], one, 0)


def go_on_kernel(groups, span, queries, *refs):
    kv, marked, state, out, scores = blocks_of(refs[:groups]), refs[-4], refs[-3], refs[-2], refs[-1]

    def one(i, carry):
        met = clips_met(kv, queries.at[i])

        @pl.when(met > 0)
        def _():
            store_state(out.at[i], visit(queries.at[i], kv, marked, scores, load_state(state.at[i]), span))

        @pl.when(met <= 0)
        def _():
            out[i] = state[i]

        return carry

    lax.fori_loop(0, queries.shape[0], one, 0)


def end_kernel(first, count, groups, span, queries, *refs):
    kv, marked, state = blocks_of(refs[:groups]), refs[groups], refs[groups + 1]
    outs, (out, last, scores) = refs[groups + 2 : -3], refs[-3:]

    def one(i, carry):
        met = clips_met(kv, queries.at[first + i])

        @pl.when(met > 0)
        def _():
            store_state(last, visit(queries.at[first + i], kv, marked, scores, load_state(state.at[first + i]), span))

        @pl.when(met <= 0)
        def _():
            last[...] = state[first + i]

        top, plain, bent = load_state(last)
        total = plain[ROWS : ROWS + 1]
        tilt = bent[WIDTH : WIDTH + 1] * SCALE
        share = 1.0 / jnp.where(total > 0, total, 1.0)
        mean_tilt = tilt * share
        mean = plain[0:WIDTH] * share
        tan_mean = (bent[0:WIDTH] * SCALE + plain[WIDTH:ROWS]) * share - mean_tilt * mean
        log_top = top * (SCALE * LOG2E)
        whole_top = jnp.maximum(jnp.ceil(log_top), -32768.0)
        weight = total * jnp.exp2(jnp.maximum(log_top - whole_top, -1.0))
        stats = [whole_top] + coded(weight, 2) + coded(mean_tilt, 2)
        for at, block in ((0, mean), (WIDTH, tan_mean)):
            code = coded(jnp.max(jnp.abs(block), axis=0, keepdims=True) * 1.0001, 1)
            stats += code
            step = FULL / jnp.maximum(decoded(code), 1e-30)
            out[i, at : at + WIDTH, :] = jnp.round(block * step).astype(jnp.int32).astype(I16)
        stats += [jnp.zeros((1, ROWS), F32)] * (META - len(stats))
        out[i, ROWS:, :] = jnp.concatenate(stats, axis=0).astype(jnp.int32).astype(I16)
        return carry

    lax.fori_loop(0, count, one, 0)
    for n in range(count):
        outs[n][0] = out[n]


def attend(queries, gathered, state=None, which=None, expect=LIGHT):
    groups, marked = gathered[:-1], gathered[-1]
    blocks = sum(group.shape[0] for group in groups)
    keys, span = blocks * ROWS, blocks // 2
    scores = pltpu.VMEM((keys, ROWS), F32)
    out_shape = jax.ShapeDtypeStruct((queries.shape[0], STATE_ROWS, ROWS), F32)
    operands, scratch, count = [queries, *groups, marked], [scores], queries.shape[0]
    if state is None:
        kernel = functools.partial(begin_kernel, len(groups), span)
    else:
        operands.append(state)
        kernel = functools.partial(go_on_kernel, len(groups), span)
    if which is not None:
        first, count = which
        kernel = functools.partial(end_kernel, first, count, len(groups), span)
        out_shape = [jax.ShapeDtypeStruct((1, Q_ROWS, ROWS), I16)] * count
        scratch = [pltpu.VMEM((count, Q_ROWS, ROWS), I16), pltpu.VMEM((STATE_ROWS, ROWS), F32), scores]
    result = pl.pallas_call(
        kernel,
        out_shape=out_shape,
        in_specs=[VMEM] * len(operands),
        out_specs=VMEM if which is None else [VMEM] * count,
        scratch_shapes=scratch,
        compiler_params=LARGE,
        cost_estimate=expect,
        name="attend",
    )(*operands)
    return result[0] if count == 1 and which is not None else result


def combine_kernel(sides, ids_ref, *refs):
    parts, (out_ref, tan_ref) = refs[:-2], refs[-2:]
    found = []
    for part in [part.at[side] for part, side in zip(parts, sides)]:
        stats = part[ROWS:, :].astype(jnp.int32).astype(F32)
        rows = [stats[r : r + 1, :] for r in range(11)]
        found.append(
            (part, rows[0], decoded(rows[1:4]), decoded(rows[4:7]), decoded(rows[7:9]), decoded(rows[9:11]))
        )
    top = functools.reduce(jnp.maximum, [f[1] for f in found])
    weights = [f[2] * jnp.exp2(f[1] - top) for f in found]
    total = functools.reduce(jnp.add, weights)
    share = 1.0 / jnp.where(total > 0, total, 1.0)
    weights = [w * share for w in weights]
    mean_tilt = functools.reduce(jnp.add, [w * f[3] for w, f in zip(weights, found)])
    result = jnp.zeros((WIDTH, ROWS), F32)
    tan_result = jnp.zeros((WIDTH, ROWS), F32)
    for weight, (part, _, _, tilt, size, tan_size) in zip(weights, found):
        mean = part[0:WIDTH, :].astype(jnp.int32).astype(F32) * (size * (1.0 / FULL))
        tan_mean = part[WIDTH : 2 * WIDTH, :].astype(jnp.int32).astype(F32) * (tan_size * (1.0 / FULL))
        result += weight * mean
        tan_result += weight * tan_mean + (weight * (tilt - mean_tilt)) * mean
    valid = ids_ref[...] < 2
    out_ref[...] = jnp.where(valid, result, 0.0).T
    tan_ref[...] = jnp.where(valid, tan_result, 0.0).T


def combine(ids, parts, sides):
    shape = jax.ShapeDtypeStruct((ROWS, WIDTH), F32)
    return pl.pallas_call(
        functools.partial(combine_kernel, sides),
        out_shape=(shape, shape),
        in_specs=[VMEM] * (1 + len(parts)),
        out_specs=(VMEM, VMEM),
        compiler_params=SMALL,
        cost_estimate=LIGHT,
        name="combine",
    )(ids.reshape(1, ROWS), *parts)


def pairs_of(move):
    return [
        (i, int(np.ravel_multi_index(move(*np.unravel_index(i, SIZES)), SIZES))) for i in range(int(np.prod(SIZES)))
    ]


def route(first, second):
    return pairs_of(lambda z, y, x, c: (second if c else first)(z, y, x) + (c,))


SIBLING = pairs_of(lambda z, y, x, c: (z, y, x, 1 - c))
RIGHT = route(*[lambda z, y, x: (z, y, (x + 1) % 4)] * 2)
LEFT = route(*[lambda z, y, x: (z, y, (x + 3) % 4)] * 2)
BOTH_WAYS = route(lambda z, y, x: (z, y, (x + 1) % 4), lambda z, y, x: (z, y, (x + 3) % 4))
LEVEL = route(*[lambda z, y, x: (1 - z, y, x)] * 2)
Q_NEXT = route(*[lambda z, y, x: (z, (y + 1) % 4, x)] * 2)
Q_LAST = route(*[lambda z, y, x: (z, (y + 3) % 4, x)] * 2)
Q_FAR = route(*[lambda z, y, x: (z, (y + 2) % 4, x)] * 2)


def back(pairs):
    return [(b, a) for a, b in pairs]


def together(*arrays):
    return lax.optimization_barrier(arrays)


def per_device(queries, keys, values, tan_queries, tan_keys, tan_values, segment_ids):
    move = functools.partial(lax.ppermute, axis_name=AXES)

    def sibling(group):
        return move(group, perm=SIBLING)

    def both(group):
        return [group, sibling(group)]

    core = lax.axis_index("core").reshape(1)
    kv, q = pack(queries, keys, values, tan_queries, tan_keys, tan_values, segment_ids)
    kv, q = kv[None], q[None]
    level = move(kv, perm=LEVEL)
    right, left = move(kv, perm=RIGHT), move(kv, perm=LEFT)
    q_next, q_last = move(q, perm=Q_NEXT), move(q, perm=Q_LAST)
    q_last, q_next, left, right, level = together(q_last, q_next, left, right, level)
    q_far = move(q, perm=Q_FAR)
    level_right, level_left = move(level, perm=RIGHT), move(level, perm=LEFT)
    first = gather(*both(kv), *both(level), *both(right), *both(left))
    near_held = stack(q_last, q_next, counts=(1, 1))
    near_state = attend(near_held, first)

    level_right, level_left, q_far, near_state = together(level_right, level_left, q_far, near_state)
    on = move(choose(core, (right, level_right), (left, level_left)), perm=BOTH_WAYS)
    more = both(level_right) + both(level_left)
    held = stack(q_far, q, counts=(1, 1))
    state = attend(held, first, expect=WAITED)
    *more, state = together(*more, state)
    second = gather(*more)
    near_state = attend(near_held, second, near_state)

    on, near_state, state = together(on, near_state, state)
    on_other = sibling(on)
    state = attend(held, second, state, expect=WAITED)
    on_other, state = together(on_other, state)
    third = gather(on, on_other)
    out_far, near_state = together(attend(held, third, state, (0, 1)), near_state)
    back_far = move(out_far, perm=back(Q_FAR))
    out_last, out_next = attend(near_held, third, near_state, (0, 2))
    back_next = move(out_next, perm=back(Q_NEXT))
    back_last = move(out_last, perm=back(Q_LAST))
    out_next, back_far, state = together(out_next, back_far, state)
    mine = attend(held, third, state, (1, 1))
    return combine(segment_ids, together(mine, back_next, back_last, back_far), (0, 0, 0, 0))


def solution(mesh):
    fine = Mesh(mesh.devices.reshape(SIZES + (2,)), AXES + ("batch",))
    rows = P(("batch",) + AXES)
    table = P(("batch",) + AXES, None)
    return jax.shard_map(
        per_device,
        mesh=fine,
        in_specs=(table,) * 6 + (rows,),
        out_specs=(table, table),
        check_vma=False,
    )
```

```python
import functools

import jax
import jax.numpy as jnp
import numpy as np
from jax import lax
from jax.experimental import pallas as pl
from jax.experimental.pallas import tpu as pltpu
from jax.sharding import Mesh, PartitionSpec as P

F32, BF16, I16 = jnp.float32, jnp.bfloat16, jnp.int16
AXES = ("z", "y", "x", "core")
SIZES = (2, 4, 4, 2)
ROWS = 256
WIDTH = 128
META = 16
KV_ROWS = 2 * ROWS + META
Q_ROWS = ROWS + META
SCALE = WIDTH**-0.5
LOG2E = 1.4426950408889634
BARRED = -(2.0**100)
UNSEEN = -(2.0**120)
STATE_ROWS = 424
FULL = 32767.0
VMEM = pl.BlockSpec(memory_space=pltpu.VMEM)
WAITED = pl.CostEstimate(flops=2 * 10**9, bytes_accessed=2**21, transcendentals=0)
LIGHT = pl.CostEstimate(flops=1, bytes_accessed=2**21, transcendentals=0)
SMALL = pltpu.CompilerParams(vmem_limit_bytes=8 * 2**20)
LARGE = pltpu.CompilerParams(vmem_limit_bytes=16 * 2**20)


def times(left, right):
    return lax.dot_general(left, right, (((1,), (0,)), ((), ())), preferred_element_type=F32)


def turned(block):
    return block.astype(F32).T.astype(BF16)


def pack_kernel(*refs):
    sources, (kv_out, q_out), held, done = refs[:7], refs[7:9], refs[9:16], refs[16]
    copies = [pltpu.make_async_copy(a, b, done.at[n]) for n, (a, b) in enumerate(zip(sources, held))]
    for copy in copies:
        copy.start()
    for copy in copies:
        copy.wait()
    q, k, v, tq, tk, tv, ids = held
    kv_out[0:ROWS, 0:WIDTH] = k[...]
    kv_out[0:ROWS, WIDTH : 2 * WIDTH] = tk[...]
    kv_out[ROWS : ROWS + WIDTH, :] = turned(v[...])
    kv_out[ROWS + WIDTH : 2 * ROWS, :] = turned(tv[...])
    q_out[0:WIDTH, :] = turned(tq[...])
    q_out[WIDTH : 2 * WIDTH, :] = turned(q[...])
    clip = ids[...]
    zeros = jnp.sum((clip == 0).astype(F32), axis=1, keepdims=True)
    ones = jnp.sum((clip == 1).astype(F32), axis=1, keepdims=True)
    row = lax.broadcasted_iota(jnp.int32, (META, ROWS), 0)
    meta = jnp.where(row == 0, zeros, jnp.where(row == 1, ones, 0.0)).astype(BF16)
    kv_out[2 * ROWS :, :] = meta
    q_out[ROWS:, :] = meta


def pack(q, k, v, tq, tk, tv, ids):
    return pl.pallas_call(
        pack_kernel,
        out_shape=(
            jax.ShapeDtypeStruct((KV_ROWS, ROWS), BF16),
            jax.ShapeDtypeStruct((Q_ROWS, ROWS), BF16),
        ),
        in_specs=[pl.BlockSpec(memory_space=pl.ANY)] * 7,
        out_specs=(VMEM, VMEM),
        scratch_shapes=[pltpu.VMEM((ROWS, WIDTH), BF16)] * 6
        + [pltpu.VMEM((1, ROWS), jnp.int32), pltpu.SemaphoreType.DMA((7,))],
        compiler_params=SMALL,
        cost_estimate=LIGHT,
        name="pack",
    )(*[pltpu.with_memory_space_constraint(a, pltpu.HBM) for a in (q, k, v, tq, tk, tv, ids.reshape(1, ROWS))])


def split(wide):
    high = wide.astype(BF16)
    return high, (wide - high.astype(F32)).astype(BF16)


def fold(wide, op):
    return op(wide.reshape(wide.shape[0] // 8, 8, wide.shape[1]), axis=0)


def key_marks(meta):
    zeros, ones = meta[0:1, 0:WIDTH], meta[1:2, 0:WIDTH]
    row = lax.broadcasted_iota(jnp.int32, (ROWS, WIDTH), 0).astype(F32)
    lane = lax.broadcasted_iota(jnp.int32, (ROWS, WIDTH), 1)
    first = row < zeros
    second = (row >= zeros) & (row < zeros + ones)
    open_ = ((lane == 0) & first) | ((lane == 1) & second) | (lane > 2)
    return jnp.where(open_, 0.0, BARRED).astype(BF16)


def query_marks(meta):
    zeros, ones = meta[0:1, :], meta[1:2, :]
    row = lax.broadcasted_iota(jnp.int32, (WIDTH, ROWS), 0)
    lane = lax.broadcasted_iota(jnp.int32, (WIDTH, ROWS), 1).astype(F32)
    clip = jnp.where(lane < zeros, 0, jnp.where(lane < zeros + ones, 1, 2))
    return jnp.where(row == clip, 1.0, 0.0).astype(BF16)


def coded(value, levels):
    size = jnp.maximum(jnp.abs(value), 1e-30)
    exponent = jnp.ceil(jnp.log2(size)) + 1.0
    left = value * jnp.exp2(-exponent) * FULL
    rows = [exponent]
    for _ in range(levels):
        digit = jnp.round(left)
        rows.append(digit)
        left = (left - digit) * FULL
    return rows


def decoded(rows):
    exponent, digits = rows[0], rows[1:]
    value = digits[-1] * (1.0 / FULL)
    for digit in digits[-2::-1]:
        value = (value + digit) * (1.0 / FULL)
    return value * jnp.exp2(exponent)


def blocks_of(refs):
    return [ref.at[n] for ref in refs for n in range(ref.shape[0])]


def choose_kernel(core, *refs):
    half = (len(refs) - 1) // 2
    for side in range(2):

        @pl.when(core[0] == side)
        def _(side=side):
            for n, block in enumerate(refs[side * half : (side + 1) * half]):
                refs[-1][n] = block[0]


def choose(core, first, second):
    return pl.pallas_call(
        choose_kernel,
        out_shape=jax.ShapeDtypeStruct((len(first),) + first[0].shape[1:], first[0].dtype),
        in_specs=[pl.BlockSpec(memory_space=pltpu.SMEM)] + [VMEM] * 2 * len(first),
        out_specs=VMEM,
        compiler_params=SMALL,
        cost_estimate=LIGHT,
        name="choose",
    )(core, *first, *second)


def stack_kernel(counts, *refs):
    at = 0
    for count, group in zip(counts, refs[:-1]):
        refs[-1][at : at + count] = group[0:count]
        at += count


def stack(*groups, counts):
    return pl.pallas_call(
        functools.partial(stack_kernel, counts),
        out_shape=jax.ShapeDtypeStruct((sum(counts),) + groups[0].shape[1:], groups[0].dtype),
        in_specs=[VMEM] * len(groups),
        out_specs=VMEM,
        compiler_params=SMALL,
        cost_estimate=LIGHT,
        name="stack",
    )(*groups)


def gather_kernel(*refs):
    blocks, kv, marked = blocks_of(refs[:-2]), refs[-2], refs[-1]
    for n, block in enumerate(blocks):
        kv[n] = block[...]
        rows = slice(n * ROWS, (n + 1) * ROWS)
        marked[rows, 0:WIDTH] = block[0:ROWS, 0:WIDTH]
        marked[rows, WIDTH:] = key_marks(block[2 * ROWS :, :].astype(F32))


def gather(*groups):
    blocks = sum(group.shape[0] for group in groups)
    return pl.pallas_call(
        gather_kernel,
        out_shape=(
            jax.ShapeDtypeStruct((blocks, KV_ROWS, ROWS), BF16),
            jax.ShapeDtypeStruct((blocks * ROWS, 2 * WIDTH), BF16),
        ),
        in_specs=[VMEM] * len(groups),
        out_specs=(VMEM, VMEM),
        compiler_params=SMALL,
        cost_estimate=LIGHT,
        name="gather",
    )(*groups)


def visit(q_block, kv, marked, scores, state, span):
    blocks = len(kv)
    q_marked = jnp.concatenate(
        [q_block[WIDTH : 2 * WIDTH, :], query_marks(q_block[ROWS:, :].astype(F32))], axis=0
    )
    q_both = q_block[0:ROWS, :]
    top = None
    for j in range(0, blocks, span):
        part = slice(j * ROWS, (j + span) * ROWS)
        own = times(marked[part], q_marked)
        scores[part] = own
        own_top = fold(own, jnp.max)
        top = own_top if top is None else jnp.maximum(top, own_top)
    top = jnp.max(top, axis=0, keepdims=True)
    if state is None:
        plain = jnp.zeros((ROWS + META, ROWS), F32)
        bent = jnp.zeros((WIDTH + META, ROWS), F32)
    else:
        old_top, plain, bent = state
        top = jnp.maximum(top, old_top)
        less = jnp.exp2((old_top - top) * (SCALE * LOG2E))
        plain, bent = plain * less, bent * less
    ones = jnp.ones((META, span * ROWS), BF16)
    for j in range(0, blocks, span):
        part = slice(j * ROWS, (j + span) * ROWS)
        group = kv[j : j + span]
        tan_scores = times(jnp.concatenate([b[0:ROWS, :] for b in group], axis=0), q_both)
        weights = jnp.exp2((scores[part] - top) * (SCALE * LOG2E))
        tilted = weights * tan_scores
        values = jnp.concatenate([b[ROWS : 2 * ROWS, :] for b in group], axis=1)
        both = jnp.concatenate([values, ones], axis=0)
        one = jnp.concatenate([values[0:WIDTH], ones], axis=0)
        high, low = split(weights)
        plain += times(both, high) + times(both, low)
        high, low = split(tilted)
        bent += times(one, high) + times(one, low)
    return top, plain, bent


def load_state(ref):
    return ref[416:417, :], ref[0:272, :], ref[272:416, :]


def store_state(ref, state):
    top, plain, bent = state
    ref[0:272, :] = plain
    ref[272:416, :] = bent
    ref[416:424, :] = jnp.broadcast_to(top, (8, ROWS))


def clips_met(kv, q_block):
    count = functools.reduce(jnp.add, [block[2 * ROWS :, :].astype(F32) for block in kv])
    return jnp.max((count * q_block[ROWS:, :].astype(F32))[0:2, :])


def begin_kernel(groups, span, queries, *refs):
    kv, marked, state, scores = blocks_of(refs[:groups]), refs[-3], refs[-2], refs[-1]

    def one(i, carry):
        met = clips_met(kv, queries.at[i])

        @pl.when(met > 0)
        def _():
            store_state(state.at[i], visit(queries.at[i], kv, marked, scores, None, span))

        @pl.when(met <= 0)
        def _():
            state[i] = jnp.zeros((STATE_ROWS, ROWS), F32)
            state[i, 416:424, :] = jnp.full((8, ROWS), UNSEEN, F32)

        return carry

    lax.fori_loop(0, queries.shape[0], one, 0)


def go_on_kernel(groups, span, queries, *refs):
    kv, marked, state, out, scores = blocks_of(refs[:groups]), refs[-4], refs[-3], refs[-2], refs[-1]

    def one(i, carry):
        met = clips_met(kv, queries.at[i])

        @pl.when(met > 0)
        def _():
            store_state(out.at[i], visit(queries.at[i], kv, marked, scores, load_state(state.at[i]), span))

        @pl.when(met <= 0)
        def _():
            out[i] = state[i]

        return carry

    lax.fori_loop(0, queries.shape[0], one, 0)


def end_kernel(first, count, groups, span, queries, *refs):
    kv, marked, state = blocks_of(refs[:groups]), refs[groups], refs[groups + 1]
    outs, (out, last, scores) = refs[groups + 2 : -3], refs[-3:]

    def one(i, carry):
        met = clips_met(kv, queries.at[first + i])

        @pl.when(met > 0)
        def _():
            store_state(last, visit(queries.at[first + i], kv, marked, scores, load_state(state.at[first + i]), span))

        @pl.when(met <= 0)
        def _():
            last[...] = state[first + i]

        top, plain, bent = load_state(last)
        total = plain[ROWS : ROWS + 1]
        tilt = bent[WIDTH : WIDTH + 1] * SCALE
        share = 1.0 / jnp.where(total > 0, total, 1.0)
        mean_tilt = tilt * share
        mean = plain[0:WIDTH] * share
        tan_mean = (bent[0:WIDTH] * SCALE + plain[WIDTH:ROWS]) * share - mean_tilt * mean
        log_top = top * (SCALE * LOG2E)
        whole_top = jnp.maximum(jnp.ceil(log_top), -32768.0)
        weight = total * jnp.exp2(jnp.maximum(log_top - whole_top, -1.0))
        stats = [whole_top] + coded(weight, 2) + coded(mean_tilt, 2)
        for at, block in ((0, mean), (WIDTH, tan_mean)):
            code = coded(jnp.max(jnp.abs(block), axis=0, keepdims=True) * 1.0001, 1)
            stats += code
            step = FULL / jnp.maximum(decoded(code), 1e-30)
            out[i, at : at + WIDTH, :] = jnp.round(block * step).astype(jnp.int32).astype(I16)
        stats += [jnp.zeros((1, ROWS), F32)] * (META - len(stats))
        out[i, ROWS:, :] = jnp.concatenate(stats, axis=0).astype(jnp.int32).astype(I16)
        return carry

    lax.fori_loop(0, count, one, 0)
    for n in range(count):
        outs[n][0] = out[n]


def attend(queries, gathered, state=None, which=None, expect=LIGHT):
    groups, marked = gathered[:-1], gathered[-1]
    blocks = sum(group.shape[0] for group in groups)
    keys, span = blocks * ROWS, blocks // 2
    scores = pltpu.VMEM((keys, ROWS), F32)
    out_shape = jax.ShapeDtypeStruct((queries.shape[0], STATE_ROWS, ROWS), F32)
    operands, scratch, count = [queries, *groups, marked], [scores], queries.shape[0]
    if state is None:
        kernel = functools.partial(begin_kernel, len(groups), span)
    else:
        operands.append(state)
        kernel = functools.partial(go_on_kernel, len(groups), span)
    if which is not None:
        first, count = which
        kernel = functools.partial(end_kernel, first, count, len(groups), span)
        out_shape = [jax.ShapeDtypeStruct((1, Q_ROWS, ROWS), I16)] * count
        scratch = [pltpu.VMEM((count, Q_ROWS, ROWS), I16), pltpu.VMEM((STATE_ROWS, ROWS), F32), scores]
    result = pl.pallas_call(
        kernel,
        out_shape=out_shape,
        in_specs=[VMEM] * len(operands),
        out_specs=VMEM if which is None else [VMEM] * count,
        scratch_shapes=scratch,
        compiler_params=LARGE,
        cost_estimate=expect,
        name="attend",
    )(*operands)
    return result[0] if count == 1 and which is not None else result


def combine_kernel(sides, ids_ref, *refs):
    parts, (out_ref, tan_ref) = refs[:-2], refs[-2:]
    found = []
    for part in [part.at[side] for part, side in zip(parts, sides)]:
        stats = part[ROWS:, :].astype(jnp.int32).astype(F32)
        rows = [stats[r : r + 1, :] for r in range(11)]
        found.append(
            (part, rows[0], decoded(rows[1:4]), decoded(rows[4:7]), decoded(rows[7:9]), decoded(rows[9:11]))
        )
    top = functools.reduce(jnp.maximum, [f[1] for f in found])
    weights = [f[2] * jnp.exp2(f[1] - top) for f in found]
    total = functools.reduce(jnp.add, weights)
    share = 1.0 / jnp.where(total > 0, total, 1.0)
    weights = [w * share for w in weights]
    mean_tilt = functools.reduce(jnp.add, [w * f[3] for w, f in zip(weights, found)])
    result = jnp.zeros((WIDTH, ROWS), F32)
    tan_result = jnp.zeros((WIDTH, ROWS), F32)
    for weight, (part, _, _, tilt, size, tan_size) in zip(weights, found):
        mean = part[0:WIDTH, :].astype(jnp.int32).astype(F32) * (size * (1.0 / FULL))
        tan_mean = part[WIDTH : 2 * WIDTH, :].astype(jnp.int32).astype(F32) * (tan_size * (1.0 / FULL))
        result += weight * mean
        tan_result += weight * tan_mean + (weight * (tilt - mean_tilt)) * mean
    valid = ids_ref[...] < 2
    out_ref[...] = jnp.where(valid, result, 0.0).T
    tan_ref[...] = jnp.where(valid, tan_result, 0.0).T


def combine(ids, parts, sides):
    shape = jax.ShapeDtypeStruct((ROWS, WIDTH), F32)
    return pl.pallas_call(
        functools.partial(combine_kernel, sides),
        out_shape=(shape, shape),
        in_specs=[VMEM] * (1 + len(parts)),
        out_specs=(VMEM, VMEM),
        compiler_params=SMALL,
        cost_estimate=LIGHT,
        name="combine",
    )(ids.reshape(1, ROWS), *parts)


def pairs_of(move):
    return [
        (i, int(np.ravel_multi_index(move(*np.unravel_index(i, SIZES)), SIZES))) for i in range(int(np.prod(SIZES)))
    ]


def route(first, second):
    return pairs_of(lambda z, y, x, c: (second if c else first)(z, y, x) + (c,))


SIBLING = pairs_of(lambda z, y, x, c: (z, y, x, 1 - c))
RIGHT = route(*[lambda z, y, x: (z, y, (x + 1) % 4)] * 2)
LEFT = route(*[lambda z, y, x: (z, y, (x + 3) % 4)] * 2)
BOTH_WAYS = route(lambda z, y, x: (z, y, (x + 1) % 4), lambda z, y, x: (z, y, (x + 3) % 4))
LEVEL = route(*[lambda z, y, x: (1 - z, y, x)] * 2)
Q_NEXT = route(*[lambda z, y, x: (z, (y + 1) % 4, x)] * 2)
Q_LAST = route(*[lambda z, y, x: (z, (y + 3) % 4, x)] * 2)
Q_FAR = route(*[lambda z, y, x: (z, (y + 2) % 4, x)] * 2)


def back(pairs):
    return [(b, a) for a, b in pairs]


def together(*arrays):
    return lax.optimization_barrier(arrays)


def per_device(queries, keys, values, tan_queries, tan_keys, tan_values, segment_ids):
    move = functools.partial(lax.ppermute, axis_name=AXES)

    def sibling(group):
        return move(group, perm=SIBLING)

    def both(group):
        return [group, sibling(group)]

    core = lax.axis_index("core").reshape(1)
    kv, q = pack(queries, keys, values, tan_queries, tan_keys, tan_values, segment_ids)
    kv, q = kv[None], q[None]
    level = move(kv, perm=LEVEL)
    right, left = move(kv, perm=RIGHT), move(kv, perm=LEFT)
    q_next, q_last = move(q, perm=Q_NEXT), move(q, perm=Q_LAST)
    q_last, q_next, left, right, level = together(q_last, q_next, left, right, level)
    q_far = move(q, perm=Q_FAR)
    level_pair = stack(*both(level), counts=(1, 1))
    level_near = move(level_pair, perm=BOTH_WAYS)
    first = gather(*both(kv), level_pair, *both(right), *both(left))
    near_held = stack(q_last, q_next, counts=(1, 1))
    near_state = attend(near_held, first)

    level_near, q_far, near_state = together(level_near, q_far, near_state)
    on = move(choose(core, (right, level_near), (left, level_near)), perm=BOTH_WAYS)
    more = both(level_near)
    held = stack(q_far, q, counts=(1, 1))
    state = attend(held, first, expect=WAITED)
    *more, state = together(*more, state)
    second = gather(*more)
    near_state = attend(near_held, second, near_state)

    on, near_state, state = together(on, near_state, state)
    on_other = sibling(on)
    state = attend(held, second, state, expect=WAITED)
    on_other, state = together(on_other, state)
    third = gather(on, on_other)
    out_far, near_state = together(attend(held, third, state, (0, 1)), near_state)
    back_far = move(out_far, perm=back(Q_FAR))
    out_last, out_next = attend(near_held, third, near_state, (0, 2))
    back_next = move(out_next, perm=back(Q_NEXT))
    back_last = move(out_last, perm=back(Q_LAST))
    out_next, back_far, state = together(out_next, back_far, state)
    mine = attend(held, third, state, (1, 1))
    return combine(segment_ids, together(mine, back_next, back_last, back_far), (0, 0, 0, 0))


def solution(mesh):
    fine = Mesh(mesh.devices.reshape(SIZES + (2,)), AXES + ("batch",))
    rows = P(("batch",) + AXES)
    table = P(("batch",) + AXES, None)
    return jax.shard_map(
        per_device,
        mesh=fine,
        in_specs=(table,) * 6 + (rows,),
        out_specs=(table, table),
        check_vma=False,
    )
```

```python
import functools

import jax
import jax.numpy as jnp
import numpy as np
from jax import lax
from jax.experimental import pallas as pl
from jax.experimental.pallas import tpu as pltpu
from jax.sharding import Mesh, PartitionSpec as P

F32, BF16, I16 = jnp.float32, jnp.bfloat16, jnp.int16
AXES = ("z", "y", "x", "core")
SIZES = (2, 4, 4, 2)
ROWS = 256
WIDTH = 128
META = 16
KV_ROWS = 2 * ROWS + META
Q_ROWS = ROWS + META
SCALE = WIDTH**-0.5
LOG2E = 1.4426950408889634
BARRED = -(2.0**100)
UNSEEN = -(2.0**120)
STATE_ROWS = 424
FULL = 32767.0
VMEM = pl.BlockSpec(memory_space=pltpu.VMEM)
WAITED = pl.CostEstimate(flops=2 * 10**9, bytes_accessed=2**21, transcendentals=0)
LIGHT = pl.CostEstimate(flops=1, bytes_accessed=2**21, transcendentals=0)
SMALL = pltpu.CompilerParams(vmem_limit_bytes=8 * 2**20)
LARGE = pltpu.CompilerParams(vmem_limit_bytes=16 * 2**20)


def times(left, right):
    return lax.dot_general(left, right, (((1,), (0,)), ((), ())), preferred_element_type=F32)


def turned(block):
    return block.astype(F32).T.astype(BF16)


def pack_kernel(*refs):
    sources, (kv_out, q_out), held, done = refs[:7], refs[7:9], refs[9:16], refs[16]
    copies = [pltpu.make_async_copy(a, b, done.at[n]) for n, (a, b) in enumerate(zip(sources, held))]
    for copy in copies:
        copy.start()
    for copy in copies:
        copy.wait()
    q, k, v, tq, tk, tv, ids = held
    kv_out[0:ROWS, 0:WIDTH] = k[...]
    kv_out[0:ROWS, WIDTH : 2 * WIDTH] = tk[...]
    kv_out[ROWS : ROWS + WIDTH, :] = turned(v[...])
    kv_out[ROWS + WIDTH : 2 * ROWS, :] = turned(tv[...])
    q_out[0:WIDTH, :] = turned(tq[...])
    q_out[WIDTH : 2 * WIDTH, :] = turned(q[...])
    clip = ids[...]
    zeros = jnp.sum((clip == 0).astype(F32), axis=1, keepdims=True)
    ones = jnp.sum((clip == 1).astype(F32), axis=1, keepdims=True)
    row = lax.broadcasted_iota(jnp.int32, (META, ROWS), 0)
    meta = jnp.where(row == 0, zeros, jnp.where(row == 1, ones, 0.0)).astype(BF16)
    kv_out[2 * ROWS :, :] = meta
    q_out[ROWS:, :] = meta


def pack(q, k, v, tq, tk, tv, ids):
    return pl.pallas_call(
        pack_kernel,
        out_shape=(
            jax.ShapeDtypeStruct((KV_ROWS, ROWS), BF16),
            jax.ShapeDtypeStruct((Q_ROWS, ROWS), BF16),
        ),
        in_specs=[pl.BlockSpec(memory_space=pl.ANY)] * 7,
        out_specs=(VMEM, VMEM),
        scratch_shapes=[pltpu.VMEM((ROWS, WIDTH), BF16)] * 6
        + [pltpu.VMEM((1, ROWS), jnp.int32), pltpu.SemaphoreType.DMA((7,))],
        compiler_params=SMALL,
        cost_estimate=LIGHT,
        name="pack",
    )(*[pltpu.with_memory_space_constraint(a, pltpu.HBM) for a in (q, k, v, tq, tk, tv, ids.reshape(1, ROWS))])


def split(wide):
    high = wide.astype(BF16)
    return high, (wide - high.astype(F32)).astype(BF16)


def fold(wide, op):
    return op(wide.reshape(wide.shape[0] // 8, 8, wide.shape[1]), axis=0)


def key_marks(meta):
    zeros, ones = meta[0:1, 0:WIDTH], meta[1:2, 0:WIDTH]
    row = lax.broadcasted_iota(jnp.int32, (ROWS, WIDTH), 0).astype(F32)
    lane = lax.broadcasted_iota(jnp.int32, (ROWS, WIDTH), 1)
    first = row < zeros
    second = (row >= zeros) & (row < zeros + ones)
    open_ = ((lane == 0) & first) | ((lane == 1) & second) | (lane > 2)
    return jnp.where(open_, 0.0, BARRED).astype(BF16)


def query_marks(meta):
    zeros, ones = meta[0:1, :], meta[1:2, :]
    row = lax.broadcasted_iota(jnp.int32, (WIDTH, ROWS), 0)
    lane = lax.broadcasted_iota(jnp.int32, (WIDTH, ROWS), 1).astype(F32)
    clip = jnp.where(lane < zeros, 0, jnp.where(lane < zeros + ones, 1, 2))
    return jnp.where(row == clip, 1.0, 0.0).astype(BF16)


def coded(value, levels):
    size = jnp.maximum(jnp.abs(value), 1e-30)
    exponent = jnp.ceil(jnp.log2(size)) + 1.0
    left = value * jnp.exp2(-exponent) * FULL
    rows = [exponent]
    for _ in range(levels):
        digit = jnp.round(left)
        rows.append(digit)
        left = (left - digit) * FULL
    return rows


def decoded(rows):
    exponent, digits = rows[0], rows[1:]
    value = digits[-1] * (1.0 / FULL)
    for digit in digits[-2::-1]:
        value = (value + digit) * (1.0 / FULL)
    return value * jnp.exp2(exponent)


def blocks_of(refs):
    return [ref.at[n] for ref in refs for n in range(ref.shape[0])]


def choose_kernel(core, *refs):
    half = (len(refs) - 1) // 2
    for side in range(2):

        @pl.when(core[0] == side)
        def _(side=side):
            for n, block in enumerate(refs[side * half : (side + 1) * half]):
                refs[-1][n] = block[0]


def choose(core, first, second):
    return pl.pallas_call(
        choose_kernel,
        out_shape=jax.ShapeDtypeStruct((len(first),) + first[0].shape[1:], first[0].dtype),
        in_specs=[pl.BlockSpec(memory_space=pltpu.SMEM)] + [VMEM] * 2 * len(first),
        out_specs=VMEM,
        compiler_params=SMALL,
        cost_estimate=LIGHT,
        name="choose",
    )(core, *first, *second)


def stack_kernel(counts, *refs):
    at = 0
    for count, group in zip(counts, refs[:-1]):
        refs[-1][at : at + count] = group[0:count]
        at += count


def stack(*groups, counts):
    return pl.pallas_call(
        functools.partial(stack_kernel, counts),
        out_shape=jax.ShapeDtypeStruct((sum(counts),) + groups[0].shape[1:], groups[0].dtype),
        in_specs=[VMEM] * len(groups),
        out_specs=VMEM,
        compiler_params=SMALL,
        cost_estimate=LIGHT,
        name="stack",
    )(*groups)


def gather_kernel(*refs):
    blocks, kv, marked = blocks_of(refs[:-2]), refs[-2], refs[-1]
    for n, block in enumerate(blocks):
        kv[n] = block[...]
        rows = slice(n * ROWS, (n + 1) * ROWS)
        marked[rows, 0:WIDTH] = block[0:ROWS, 0:WIDTH]
        marked[rows, WIDTH:] = key_marks(block[2 * ROWS :, :].astype(F32))


def gather(*groups):
    blocks = sum(group.shape[0] for group in groups)
    return pl.pallas_call(
        gather_kernel,
        out_shape=(
            jax.ShapeDtypeStruct((blocks, KV_ROWS, ROWS), BF16),
            jax.ShapeDtypeStruct((blocks * ROWS, 2 * WIDTH), BF16),
        ),
        in_specs=[VMEM] * len(groups),
        out_specs=(VMEM, VMEM),
        compiler_params=SMALL,
        cost_estimate=LIGHT,
        name="gather",
    )(*groups)


def visit(q_block, kv, marked, scores, state, span):
    blocks = len(kv)
    q_marked = jnp.concatenate(
        [q_block[WIDTH : 2 * WIDTH, :], query_marks(q_block[ROWS:, :].astype(F32))], axis=0
    )
    q_both = q_block[0:ROWS, :]
    top = None
    for j in range(0, blocks, span):
        part = slice(j * ROWS, (j + span) * ROWS)
        own = times(marked[part], q_marked)
        scores[part] = own
        own_top = fold(own, jnp.max)
        top = own_top if top is None else jnp.maximum(top, own_top)
    top = jnp.max(top, axis=0, keepdims=True)
    if state is None:
        plain = jnp.zeros((ROWS + META, ROWS), F32)
        bent = jnp.zeros((WIDTH + META, ROWS), F32)
    else:
        old_top, plain, bent = state
        top = jnp.maximum(top, old_top)
        less = jnp.exp2((old_top - top) * (SCALE * LOG2E))
        plain, bent = plain * less, bent * less
    ones = jnp.ones((META, span * ROWS), BF16)
    for j in range(0, blocks, span):
        part = slice(j * ROWS, (j + span) * ROWS)
        group = kv[j : j + span]
        tan_scores = times(jnp.concatenate([b[0:ROWS, :] for b in group], axis=0), q_both)
        weights = jnp.exp2((scores[part] - top) * (SCALE * LOG2E))
        tilted = weights * tan_scores
        values = jnp.concatenate([b[ROWS : 2 * ROWS, :] for b in group], axis=1)
        both = jnp.concatenate([values, ones], axis=0)
        one = jnp.concatenate([values[0:WIDTH], ones], axis=0)
        high, low = split(weights)
        plain += times(both, high) + times(both, low)
        high, low = split(tilted)
        bent += times(one, high) + times(one, low)
    return top, plain, bent


def load_state(ref):
    return ref[416:417, :], ref[0:272, :], ref[272:416, :]


def store_state(ref, state):
    top, plain, bent = state
    ref[0:272, :] = plain
    ref[272:416, :] = bent
    ref[416:424, :] = jnp.broadcast_to(top, (8, ROWS))


def clips_met(kv, q_block):
    count = functools.reduce(jnp.add, [block[2 * ROWS :, :].astype(F32) for block in kv])
    return jnp.max((count * q_block[ROWS:, :].astype(F32))[0:2, :])


def begin_kernel(groups, span, queries, *refs):
    kv, marked, state, scores = blocks_of(refs[:groups]), refs[-3], refs[-2], refs[-1]

    def one(i, carry):
        met = clips_met(kv, queries.at[i])

        @pl.when(met > 0)
        def _():
            store_state(state.at[i], visit(queries.at[i], kv, marked, scores, None, span))

        @pl.when(met <= 0)
        def _():
            state[i] = jnp.zeros((STATE_ROWS, ROWS), F32)
            state[i, 416:424, :] = jnp.full((8, ROWS), UNSEEN, F32)

        return carry

    lax.fori_loop(0, queries.shape[0], one, 0)


def go_on_kernel(groups, span, queries, *refs):
    kv, marked, state, out, scores = blocks_of(refs[:groups]), refs[-4], refs[-3], refs[-2], refs[-1]

    def one(i, carry):
        met = clips_met(kv, queries.at[i])

        @pl.when(met > 0)
        def _():
            store_state(out.at[i], visit(queries.at[i], kv, marked, scores, load_state(state.at[i]), span))

        @pl.when(met <= 0)
        def _():
            out[i] = state[i]

        return carry

    lax.fori_loop(0, queries.shape[0], one, 0)


def end_kernel(first, count, groups, span, queries, *refs):
    kv, marked, state = blocks_of(refs[:groups]), refs[groups], refs[groups + 1]
    outs, (out, last, scores) = refs[groups + 2 : -3], refs[-3:]

    def one(i, carry):
        met = clips_met(kv, queries.at[first + i])

        @pl.when(met > 0)
        def _():
            store_state(last, visit(queries.at[first + i], kv, marked, scores, load_state(state.at[first + i]), span))

        @pl.when(met <= 0)
        def _():
            last[...] = state[first + i]

        top, plain, bent = load_state(last)
        total = plain[ROWS : ROWS + 1]
        tilt = bent[WIDTH : WIDTH + 1] * SCALE
        share = 1.0 / jnp.where(total > 0, total, 1.0)
        mean_tilt = tilt * share
        mean = plain[0:WIDTH] * share
        tan_mean = (bent[0:WIDTH] * SCALE + plain[WIDTH:ROWS]) * share - mean_tilt * mean
        log_top = top * (SCALE * LOG2E)
        whole_top = jnp.maximum(jnp.ceil(log_top), -32768.0)
        weight = total * jnp.exp2(jnp.maximum(log_top - whole_top, -1.0))
        stats = [whole_top] + coded(weight, 2) + coded(mean_tilt, 2)
        for at, block in ((0, mean), (WIDTH, tan_mean)):
            code = coded(jnp.max(jnp.abs(block), axis=0, keepdims=True) * 1.0001, 1)
            stats += code
            step = FULL / jnp.maximum(decoded(code), 1e-30)
            out[i, at : at + WIDTH, :] = jnp.round(block * step).astype(jnp.int32).astype(I16)
        stats += [jnp.zeros((1, ROWS), F32)] * (META - len(stats))
        out[i, ROWS:, :] = jnp.concatenate(stats, axis=0).astype(jnp.int32).astype(I16)
        return carry

    lax.fori_loop(0, count, one, 0)
    for n in range(count):
        outs[n][0] = out[n]


def attend(queries, gathered, state=None, which=None, expect=LIGHT):
    groups, marked = gathered[:-1], gathered[-1]
    blocks = sum(group.shape[0] for group in groups)
    keys, span = blocks * ROWS, blocks // 2
    scores = pltpu.VMEM((keys, ROWS), F32)
    out_shape = jax.ShapeDtypeStruct((queries.shape[0], STATE_ROWS, ROWS), F32)
    operands, scratch, count = [queries, *groups, marked], [scores], queries.shape[0]
    if state is None:
        kernel = functools.partial(begin_kernel, len(groups), span)
    else:
        operands.append(state)
        kernel = functools.partial(go_on_kernel, len(groups), span)
    if which is not None:
        first, count = which
        kernel = functools.partial(end_kernel, first, count, len(groups), span)
        out_shape = [jax.ShapeDtypeStruct((1, Q_ROWS, ROWS), I16)] * count
        scratch = [pltpu.VMEM((count, Q_ROWS, ROWS), I16), pltpu.VMEM((STATE_ROWS, ROWS), F32), scores]
    result = pl.pallas_call(
        kernel,
        out_shape=out_shape,
        in_specs=[VMEM] * len(operands),
        out_specs=VMEM if which is None else [VMEM] * count,
        scratch_shapes=scratch,
        compiler_params=LARGE,
        cost_estimate=expect,
        name="attend",
    )(*operands)
    return result[0] if count == 1 and which is not None else result


def combine_kernel(sides, ids_ref, *refs):
    parts, (out_ref, tan_ref) = refs[:-2], refs[-2:]
    found = []
    for part in [part.at[side] for part, side in zip(parts, sides)]:
        stats = part[ROWS:, :].astype(jnp.int32).astype(F32)
        rows = [stats[r : r + 1, :] for r in range(11)]
        found.append(
            (part, rows[0], decoded(rows[1:4]), decoded(rows[4:7]), decoded(rows[7:9]), decoded(rows[9:11]))
        )
    top = functools.reduce(jnp.maximum, [f[1] for f in found])
    weights = [f[2] * jnp.exp2(f[1] - top) for f in found]
    total = functools.reduce(jnp.add, weights)
    share = 1.0 / jnp.where(total > 0, total, 1.0)
    weights = [w * share for w in weights]
    mean_tilt = functools.reduce(jnp.add, [w * f[3] for w, f in zip(weights, found)])
    result = jnp.zeros((WIDTH, ROWS), F32)
    tan_result = jnp.zeros((WIDTH, ROWS), F32)
    for weight, (part, _, _, tilt, size, tan_size) in zip(weights, found):
        mean = part[0:WIDTH, :].astype(jnp.int32).astype(F32)
        tan_mean = part[WIDTH : 2 * WIDTH, :].astype(jnp.int32).astype(F32)
        factor = weight * (size * (1.0 / FULL))
        tan_factor = weight * (tan_size * (1.0 / FULL))
        result += factor * mean
        tan_result += tan_factor * tan_mean + (factor * (tilt - mean_tilt)) * mean
    valid = ids_ref[...] < 2
    out_ref[...] = jnp.where(valid, result, 0.0).T
    tan_ref[...] = jnp.where(valid, tan_result, 0.0).T


def combine(ids, parts, sides):
    shape = jax.ShapeDtypeStruct((ROWS, WIDTH), F32)
    return pl.pallas_call(
        functools.partial(combine_kernel, sides),
        out_shape=(shape, shape),
        in_specs=[VMEM] * (1 + len(parts)),
        out_specs=(VMEM, VMEM),
        compiler_params=SMALL,
        cost_estimate=LIGHT,
        name="combine",
    )(ids.reshape(1, ROWS), *parts)


def pairs_of(move):
    return [
        (i, int(np.ravel_multi_index(move(*np.unravel_index(i, SIZES)), SIZES))) for i in range(int(np.prod(SIZES)))
    ]


def route(first, second):
    return pairs_of(lambda z, y, x, c: (second if c else first)(z, y, x) + (c,))


SIBLING = pairs_of(lambda z, y, x, c: (z, y, x, 1 - c))
RIGHT = route(*[lambda z, y, x: (z, y, (x + 1) % 4)] * 2)
LEFT = route(*[lambda z, y, x: (z, y, (x + 3) % 4)] * 2)
BOTH_WAYS = route(lambda z, y, x: (z, y, (x + 1) % 4), lambda z, y, x: (z, y, (x + 3) % 4))
LEVEL = route(*[lambda z, y, x: (1 - z, y, x)] * 2)
Q_NEXT = route(*[lambda z, y, x: (z, (y + 1) % 4, x)] * 2)
Q_LAST = route(*[lambda z, y, x: (z, (y + 3) % 4, x)] * 2)
Q_FAR = route(*[lambda z, y, x: (z, (y + 2) % 4, x)] * 2)


def back(pairs):
    return [(b, a) for a, b in pairs]


def together(*arrays):
    return lax.optimization_barrier(arrays)


def per_device(queries, keys, values, tan_queries, tan_keys, tan_values, segment_ids):
    move = functools.partial(lax.ppermute, axis_name=AXES)

    def sibling(group):
        return move(group, perm=SIBLING)

    def both(group):
        return [group, sibling(group)]

    core = lax.axis_index("core").reshape(1)
    kv, q = pack(queries, keys, values, tan_queries, tan_keys, tan_values, segment_ids)
    kv, q = kv[None], q[None]
    level = move(kv, perm=LEVEL)
    right, left = move(kv, perm=RIGHT), move(kv, perm=LEFT)
    q_next, q_last = move(q, perm=Q_NEXT), move(q, perm=Q_LAST)
    q_last, q_next, left, right, level = together(q_last, q_next, left, right, level)
    q_far = move(q, perm=Q_FAR)
    level_pair = stack(*both(level), counts=(1, 1))
    level_near = move(level_pair, perm=BOTH_WAYS)
    first = gather(*both(kv), level_pair, *both(right), *both(left))
    near_held = stack(q_last, q_next, counts=(1, 1))
    near_state = attend(near_held, first)

    level_near, q_far, near_state = together(level_near, q_far, near_state)
    on = move(choose(core, (right, level_near), (left, level_near)), perm=BOTH_WAYS)
    more = both(level_near)
    held = stack(q_far, q, counts=(1, 1))
    state = attend(held, first, expect=WAITED)
    *more, state = together(*more, state)
    second = gather(*more)
    near_state = attend(near_held, second, near_state)

    on, near_state, state = together(on, near_state, state)
    on_other = sibling(on)
    state = attend(held, second, state, expect=WAITED)
    on_other, state = together(on_other, state)
    third = gather(on, on_other)
    out_far, near_state = together(attend(held, third, state, (0, 1)), near_state)
    back_far = move(out_far, perm=back(Q_FAR))
    out_last, out_next = attend(near_held, third, near_state, (0, 2))
    back_next = move(out_next, perm=back(Q_NEXT))
    back_last = move(out_last, perm=back(Q_LAST))
    out_next, back_far, state = together(out_next, back_far, state)
    mine = attend(held, third, state, (1, 1))
    return combine(segment_ids, together(mine, back_next, back_last, back_far), (0, 0, 0, 0))


def solution(mesh):
    fine = Mesh(mesh.devices.reshape(SIZES + (2,)), AXES + ("batch",))
    rows = P(("batch",) + AXES)
    table = P(("batch",) + AXES, None)
    return jax.shard_map(
        per_device,
        mesh=fine,
        in_specs=(table,) * 6 + (rows,),
        out_specs=(table, table),
        check_vma=False,
    )
```
